256 devices in a mesh: lon: 32 (over z_lo, x, core), lat: 8 (over z_hi, y).
Axes of the slice: x: 4, y: 4, z: 8 (z_hi: 2, z_lo: 4; z = z_hi * 4 + z_lo), core: 2. Of those that a mesh axis runs over, the one named last changes fastest.
Arguments:
- warmth_anomaly: float32 [16, 256, 4096], P(None, 'lat', 'lon'), may hold values from -6 to 6
- brine_anomaly: float32 [16, 256, 4096], P(None, 'lat', 'lon'), may hold values from -6 to 6
- zonal_speed: float32 [16, 256, 4096], P(None, 'lat', 'lon'), may hold values from -3 to 3
- meridional_speed: float32 [16, 256, 4096], P(None, 'lat', 'lon'), may hold values from -3 to 3
- upper_bound_stress: float32 [256, 4096], P('lat', 'lon'), may hold values from -6 to 6
- sea_indicator: int32 [16, 256, 4096], P(None, 'lat', 'lon'), may hold values 0 or 1
Outputs:
- temperature_out: float32 [16, 256, 4096], P(None, 'lat', 'lon')
- salinity_out: float32 [16, 256, 4096], P(None, 'lat', 'lon')
- zonal_out: float32 [16, 256, 4096], P(None, 'lat', 'lon')
- meridional_out: float32 [16, 256, 4096], P(None, 'lat', 'lon')
- pressure_out: float32 [16, 256, 4096], P(None, 'lat', 'lon')
The draws below stay inside these ranges and needn't reach their ends.
All inputs are finite; a program needn't handle non-finite values. No bound on the sum of `sea_indicator` on one device may be relied on, other than what follows from the above.
Results may differ from the reference program's by a relative error of at most 0.00002.
Values sent between devices are 32-bit elements; how exact they have to be, the bound alone decides.
No kernel may reach another device: no remote copies, remote signals or barrier semaphores. Data moves between devices by JAX's collectives and lax.ppermute only.
A program may use at most 64 MiB of HBM per device.

```python
import jax
import jax.numpy as jnp

VERTICAL_STRATA = 16
STEPS = 2
MERIDIAN_POINTS = 256
PARALLEL_POINTS = 4096


def touch_ends(result, own_key, low, high):
    index_at = [jax.random.randint(jax.random.fold_in(own_key, axis), (), 0, length) for axis, length in enumerate(result.shape)]
    longest = result.shape.index(max(result.shape))
    neighbour = index_at[:longest] + [(index_at[longest] + 1) % result.shape[longest]] + index_at[longest + 1:]
    return result.at[tuple(index_at)].set(low).at[tuple(neighbour)].set(high)


def steps_of(key, dims, split, low, largest):
    loudness = 1.0
    for dim, blocks in split:
        draws = jax.random.uniform(jax.random.fold_in(jax.random.fold_in(key, 6), dim), (blocks,), jnp.float32, low / len(split), largest / len(split))
        loudness = loudness * jnp.repeat(jnp.exp(draws), dims[dim] // blocks).reshape((-1,) + (1,) * (len(dims) - 1 - dim))
    return loudness


def scatter_about(stream_key, shape, deviation, limit, pieces=(), kind=jnp.bfloat16):
    level = steps_of(stream_key, shape, pieces, -0.22, 0.18) if pieces else 1.0
    entries = jax.random.normal(stream_key, shape, jnp.float32) * deviation * level
    return jnp.minimum(jnp.maximum(entries, -limit), limit).astype(kind)


def setup_inputs(seed: int = 0) -> dict:
    streams_of = jax.random.split(jax.random.key(seed), 7)
    return {
        "warmth_anomaly": scatter_about(streams_of[0], (VERTICAL_STRATA, MERIDIAN_POINTS, PARALLEL_POINTS), 1.0, 6.0, ((1, 8), (2, 32)), jnp.float32),
        "brine_anomaly": scatter_about(streams_of[1], (VERTICAL_STRATA, MERIDIAN_POINTS, PARALLEL_POINTS), 1.0, 6.0, ((1, 8), (2, 32)), jnp.float32),
        "zonal_speed": scatter_about(streams_of[2], (VERTICAL_STRATA, MERIDIAN_POINTS, PARALLEL_POINTS), 0.5, 3.0, ((1, 8), (2, 32)), jnp.float32),
        "meridional_speed": scatter_about(streams_of[3], (VERTICAL_STRATA, MERIDIAN_POINTS, PARALLEL_POINTS), 0.5, 3.0, ((1, 8), (2, 32)), jnp.float32),
        "upper_bound_stress": scatter_about(streams_of[4], (MERIDIAN_POINTS, PARALLEL_POINTS), 1.0, 6.0, ((0, 8), (1, 32)), jnp.float32),
        "sea_indicator": touch_ends((jax.random.randint(streams_of[5], (VERTICAL_STRATA, MERIDIAN_POINTS, PARALLEL_POINTS), 0, 4) < 3).astype(jnp.int32), jax.random.fold_in(streams_of[5], 1), 0, 1),
    }


HEAT_EXPANSION = 0.2
SALT_CONTRACTION = 0.15
GRAVITY = 0.5
TIME_STEP = 0.2
VISCOSITY = 0.25
DIFFUSIVITY = 0.2
ROTATION = 1.0


def stratum_stress(warmth_anomaly, brine_anomaly, uppermost_stratum):
    seawater_heaviness = -HEAT_EXPANSION * warmth_anomaly + SALT_CONTRACTION * brine_anomaly
    overlying = jnp.cumsum(seawater_heaviness, axis=0) - seawater_heaviness
    return uppermost_stratum + GRAVITY * (overlying + 0.5 * seawater_heaviness)


def neighbours(field):
    return (field[:, 1:-1, 1:-1], field[:, 1:-1, 2:], field[:, 1:-1, :-2], field[:, 2:, 1:-1], field[:, :-2, 1:-1])


def laplace(parts):
    return parts[1] + parts[2] + parts[3] + parts[4] - 4.0 * parts[0]


def march_forward(temp_wide, salt_wide, zonal_wide, merid_wide, press_wide, wet_mask, coriolis):
    zonal = neighbours(zonal_wide)
    merid = neighbours(merid_wide)
    hydro_stress = neighbours(press_wide)
    easterly_speed_current = zonal[0]
    northerly_speed_current = merid[0]
    grad_x = 0.5 * (hydro_stress[1] - hydro_stress[2])
    grad_y = 0.5 * (hydro_stress[3] - hydro_stress[4])
    zonal_next = wet_mask * (easterly_speed_current + TIME_STEP * (coriolis * northerly_speed_current - grad_x + VISCOSITY * laplace(zonal)))
    merid_next = wet_mask * (northerly_speed_current + TIME_STEP * (-coriolis * easterly_speed_current - grad_y + VISCOSITY * laplace(merid)))

    def tracer(wide_field):
        parts = neighbours(wide_field)
        transport = -0.5 * (easterly_speed_current * (parts[1] - parts[2]) + northerly_speed_current * (parts[3] - parts[4]))
        return wet_mask * (parts[0] + TIME_STEP * (transport + DIFFUSIVITY * laplace(parts)))

    return tracer(temp_wide), tracer(salt_wide), zonal_next, merid_next


def pad_borders(field, flip):
    east_west = jnp.concatenate([field[..., -1:], field, field[..., :1]], axis=-1)
    northern = flip * field[:, -1:, ::-1]
    northern = jnp.pad(northern, ((0, 0), (0, 0), (1, 1)))
    southern = jnp.zeros_like(northern)
    return jnp.concatenate([southern, east_west, northern], axis=1)


def reference(warmth_anomaly, brine_anomaly, zonal_speed, meridional_speed, upper_bound_stress, sea_indicator):
    wet_mask = sea_indicator.astype(jnp.float32)
    row_index = jnp.arange(MERIDIAN_POINTS).astype(jnp.float32)
    coriolis = (ROTATION * ((2.0 * (row_index + 0.5)) / MERIDIAN_POINTS - 1.0))[:, None]
    existing_warmth, existing_brine = warmth_anomaly, brine_anomaly
    easterly_speed_current, northerly_speed_current = zonal_speed, meridional_speed
    for step_index in range(STEPS):
        hydro_stress = stratum_stress(existing_warmth, existing_brine, upper_bound_stress)
        existing_warmth, existing_brine, easterly_speed_current, northerly_speed_current = march_forward(
            pad_borders(existing_warmth, 1.0), pad_borders(existing_brine, 1.0), pad_borders(easterly_speed_current, -1.0),
            pad_borders(northerly_speed_current, -1.0), pad_borders(hydro_stress, 1.0), wet_mask, coriolis)
    ending_stress = stratum_stress(existing_warmth, existing_brine, upper_bound_stress)
    return existing_warmth, existing_brine, easterly_speed_current, northerly_speed_current, ending_stress
```

```python
import jax
import jax.numpy as jnp
from jax import lax
from jax.experimental import pallas as pl
from jax.experimental.pallas import tpu as pltpu
from jax.sharding import PartitionSpec as P

STEPS = 2
HEAT_EXPANSION = 0.2
SALT_CONTRACTION = 0.15
GRAVITY = 0.5
TIME_STEP = 0.2
VISCOSITY = 0.25
DIFFUSIVITY = 0.2
ROTATION = 1.0

LEVELS = 16
ROWS = 32
LANES = 128
BLOCKS = ROWS // 8
SLOTS = LEVELS * BLOCKS

COL_T, COL_S, COL_U, COL_V, COL_WET, COL_PS = range(6)
COL_TILE = 8
COL_ROWS = 6 * COL_TILE
ROW_WET = 4 * 2 * LEVELS
ROW_PS = ROW_WET + LEVELS
ROW_CORNER = ROW_PS + 8
ROW_ROWS = ROW_CORNER + 8

FIRST = 16
EXT_ROWS = 64
EXT_LANES = 2 * LANES

VMEM = pl.BlockSpec(memory_space=pltpu.VMEM)


def lanes_of(shape):
    return lax.broadcasted_iota(jnp.int32, shape, len(shape) - 1)


def pack_columns(t_ref, s_ref, u_ref, v_ref, ps_ref, wet_ref, near_ref, far_ref):
    even = lax.axis_index("lon") % 2 == 0
    slot = lanes_of((8, LANES)) >> 1
    masks = [slot == j for j in range(SLOTS)]

    def pack(index, tiles):
        east = jnp.zeros((8, LANES), jnp.float32)
        west = jnp.zeros((8, LANES), jnp.float32)
        for j, tile in enumerate(tiles):
            rolled = pltpu.roll(tile(), (2 * j + 2) % LANES, 1)
            east = jnp.where(masks[j], rolled, east)
            west = jnp.where(masks[(j + 1) % SLOTS], rolled, west)
        rows = pl.ds(index * COL_TILE, COL_TILE)
        near_ref[rows, :] = jnp.where(even, east, west)
        far_ref[rows, :] = jnp.where(even, west, east)

    def tiles_of(ref):
        return [
            (lambda j=j: ref[j // BLOCKS, pl.ds(8 * (j % BLOCKS), 8), :].astype(jnp.float32))
            for j in range(SLOTS)
        ]

    for index, ref in ((COL_T, t_ref), (COL_S, s_ref), (COL_U, u_ref), (COL_V, v_ref), (COL_WET, wet_ref)):
        pack(index, tiles_of(ref))
    pack(COL_PS, [(lambda r=r: ps_ref[pl.ds(8 * r, 8), :]) for r in range(BLOCKS)])


def reverse_lanes(value):
    index = LANES - 1 - lanes_of(value.shape)
    return jnp.take_along_axis(value, index, axis=1, mode="promise_in_bounds")


def pack_rows(t_ref, s_ref, u_ref, v_ref, ps_ref, wet_ref, near_ref, far_ref):
    lat = lax.axis_index("lat")
    even = lat % 2 == 0
    fold = lat == lax.axis_size("lat") - 1

    def put(first, north, south, sign):
        rows = pl.ds(first, north.shape[0])
        near_ref[rows, :] = jnp.where(even, north, south)
        far_ref[rows, :] = jnp.where(even, south, north)

        @pl.when(fold)
        def _():
            far_ref[rows, :] = sign * reverse_lanes(north)

    for index, (ref, sign) in enumerate(((t_ref, 1.0), (s_ref, 1.0), (u_ref, -1.0), (v_ref, -1.0))):
        for ring in range(2):
            put(
                (2 * index + ring) * LEVELS,
                ref[:, ROWS - 1 - ring, :],
                ref[:, ring, :],
                sign,
            )
    put(ROW_WET, wet_ref[:, ROWS - 1, :].astype(jnp.float32), wet_ref[:, 0, :].astype(jnp.float32), 1.0)
    top, bottom = ps_ref[pl.ds(ROWS - 8, 8), :], ps_ref[pl.ds(0, 8), :]
    sub = lax.broadcasted_iota(jnp.int32, (8, LANES), 0)
    north = jnp.where(sub == 0, pltpu.roll(top, 1, 0), pltpu.roll(top, 3, 0))
    put(ROW_PS, north, bottom, 1.0)
    near_ref[pl.ds(ROW_CORNER, 8), :] = jnp.zeros((8, LANES), jnp.float32)
    far_ref[pl.ds(ROW_CORNER, 8), :] = jnp.zeros((8, LANES), jnp.float32)


def halo_tiles(near, far, even_lon):
    slot = lanes_of(near.shape) >> 1
    west = jnp.where(even_lon, far, near)
    east = jnp.where(even_lon, near, far)
    return (
        jnp.where(slot % 2 == 0, west, east),
        jnp.where(slot % 2 == 0, east, west),
    )


def pack_corners(near_ref, far_ref, near_out, far_out):
    lat = lax.axis_index("lat")
    even = lat % 2 == 0
    fold = lat == lax.axis_size("lat") - 1
    even_tile, odd_tile = halo_tiles(near_ref[...], far_ref[...], lax.axis_index("lon") % 2 == 0)
    lane = lanes_of((8, LANES))
    sub = lax.broadcasted_iota(jnp.int32, (8, LANES), 0)

    def gather(tile, row):
        out = jnp.zeros((8, LANES), jnp.float32)
        for index, field in enumerate((COL_T, COL_S, COL_U, COL_V, COL_PS)):
            one = pltpu.roll(tile[field * COL_TILE : (field + 1) * COL_TILE], (index - row) % 8, 0)
            out = jnp.where(sub == index, one, out)
        return out

    north, south = gather(odd_tile, 7), gather(even_tile, 0)
    mirrored = pltpu.roll(north, LANES - 6, 1)
    mirrored = jnp.where(lane % 2 == 0, pltpu.roll(mirrored, 1, 1), pltpu.roll(mirrored, LANES - 1, 1))
    mirrored = jnp.where((sub == 2) | (sub == 3), -mirrored, mirrored)
    near_out[...] = jnp.where(even, north, south)
    far_out[...] = jnp.where(fold, mirrored, jnp.where(even, south, north))


def step_kernel(
    t_ref, s_ref, u_ref, v_ref, ps_ref, wet_ref, col_near_ref, col_far_ref, row_near_ref, row_far_ref,
    t_out, s_out, u_out, v_out, p_out,
    x_ref, w_ref, psx_ref, p_ref, y_ref,
):
    lat = lax.axis_index("lat")
    lat_count = lax.axis_size("lat")
    even = lat % 2 == 0
    even_tile, odd_tile = halo_tiles(
        col_near_ref[...], col_far_ref[...], lax.axis_index("lon") % 2 == 0
    )
    fields = (t_ref, s_ref, u_ref, v_ref)
    own = pl.ds(FIRST, ROWS)
    inner, halo = pl.ds(0, LANES), pl.ds(LANES, LANES)

    def tile_of(index, j):
        tile = (odd_tile if j % 2 else even_tile)[index * COL_TILE : (index + 1) * COL_TILE]
        return pltpu.roll(tile, (-2 * (j + 1)) % LANES, 1)

    def copy_level(k, _):
        for index, ref in enumerate(fields):
            x_ref[index, k, own, inner] = ref[k]
        w_ref[k, own, inner] = wet_ref[k].astype(jnp.float32)
        return 0

    lax.fori_loop(0, LEVELS, copy_level, 0)
    psx_ref[own, inner] = ps_ref[...]
    for j in range(SLOTS):
        k, rows = j // BLOCKS, pl.ds(FIRST + 8 * (j % BLOCKS), 8)
        for index in range(4):
            x_ref[index, k, rows, halo] = tile_of(index, j)
        w_ref[k, rows, halo] = tile_of(COL_WET, j)
        if k == 0:
            psx_ref[rows, halo] = tile_of(COL_PS, j)

    near, far = row_near_ref[...], row_far_ref[...]
    south = jnp.where(even, far, near)
    south = jnp.where(lat == 0, 0.0, south)
    north = jnp.where(even, near, far)
    for value, first, away, block in ((south, FIRST - 1, -1, BLOCKS - 1), (north, FIRST + ROWS, 1, 0)):
        for k in range(LEVELS):
            shift = (-2 * (BLOCKS * k + block + 1)) % LANES
            for index in range(4):
                for ring in range(2):
                    at = (2 * index + ring) * LEVELS + k
                    x_ref[index, k, pl.ds(first + away * ring, 1), inner] = value[at : at + 1]
                corner = value[ROW_CORNER + index : ROW_CORNER + index + 1]
                x_ref[index, k, pl.ds(first, 1), halo] = pltpu.roll(corner, shift, 1)
            w_ref[k, pl.ds(first, 1), inner] = value[ROW_WET + k : ROW_WET + k + 1]
        for ring in range(2):
            psx_ref[pl.ds(first + away * ring, 1), inner] = value[ROW_PS + ring : ROW_PS + ring + 1]
        corner = value[ROW_CORNER + 4 : ROW_CORNER + 5]
        psx_ref[pl.ds(first, 1), halo] = pltpu.roll(corner, (-2 * (block + 1)) % LANES, 1)

    def pressure(src, lo, count, lanes, put):
        rows = pl.ds(lo, count)
        psv = psx_ref[rows, lanes]

        def level(k, running):
            heavy = -HEAT_EXPANSION * src[0, k, rows, lanes] + SALT_CONTRACTION * src[1, k, rows, lanes]
            put(k, psv + GRAVITY * (running + 0.5 * heavy))
            return running + heavy

        lax.fori_loop(0, LEVELS, level, jnp.zeros_like(psv))

    def put_p(k, value):
        p_ref[k, pl.ds(8, 48), :] = value

    def march(src, k, base, wide, put):
        lanes = pl.ds(0, EXT_LANES)

        def parts(ref, *lead):
            centre = ref[(*lead, k, pl.ds(base, 8), lanes)]
            east = pltpu.roll(centre, EXT_LANES - 1, 1)
            west = pltpu.roll(centre, 1, 1)
            if not wide:
                centre, east, west = (q[:, :LANES] for q in (centre, east, west))
            across = lanes if wide else inner
            return (
                centre,
                east,
                west,
                ref[(*lead, k, pl.ds(base + 1, 8), across)],
                ref[(*lead, k, pl.ds(base - 1, 8), across)],
            )

        def laplace(q):
            return q[1] + q[2] + q[3] + q[4] - 4.0 * q[0]

        row = base - FIRST + lax.broadcasted_iota(jnp.int32, (8, EXT_LANES if wide else LANES), 0)
        row = lat * ROWS + row
        row = jnp.minimum(row, lat_count * ROWS - 1).astype(jnp.float32)
        coriolis = ROTATION * (2.0 * (row + 0.5) / (lat_count * ROWS) - 1.0)
        wet = w_ref[k, pl.ds(base, 8), lanes if wide else inner]
        u, v = parts(src, 2), parts(src, 3)
        p = parts(p_ref)
        grad_x = 0.5 * (p[1] - p[2])
        grad_y = 0.5 * (p[3] - p[4])
        put(2, wet * (u[0] + TIME_STEP * (coriolis * v[0] - grad_x + VISCOSITY * laplace(u))))
        put(3, wet * (v[0] + TIME_STEP * (-coriolis * u[0] - grad_y + VISCOSITY * laplace(v))))
        for index in range(2):
            q = parts(src, index)
            transport = -0.5 * (u[0] * (q[1] - q[2]) + v[0] * (q[3] - q[4]))
            put(index, wet * (q[0] + TIME_STEP * (transport + DIFFUSIVITY * laplace(q))))

    everywhere = pl.ds(0, EXT_LANES)
    pressure(x_ref, 8, 48, everywhere, put_p)

    def first_step(k, _):
        for base in range(8, 56, 8):
            def put(index, value, base=base):
                y_ref[index, k, pl.ds(base, 8), :] = value

            march(x_ref, k, base, True, put)
        return 0

    lax.fori_loop(0, LEVELS, first_step, 0)
    pressure(y_ref, 8, 48, everywhere, put_p)
    outs = (t_out, s_out, u_out, v_out)

    def second_step(k, _):
        for block in range(BLOCKS):
            def put(index, value, block=block):
                outs[index][k, pl.ds(8 * block, 8), :] = value

            march(y_ref, k, FIRST + 8 * block, False, put)
        return 0

    lax.fori_loop(0, LEVELS, second_step, 0)
    psv = ps_ref[...]

    def last(k, running):
        heavy = -HEAT_EXPANSION * t_out[k] + SALT_CONTRACTION * s_out[k]
        p_out[k] = psv + GRAVITY * (running + 0.5 * heavy)
        return running + heavy

    lax.fori_loop(0, LEVELS, last, jnp.zeros_like(psv))


def exchanges(lon_count, lat_count):
    def at(lat, lon):
        return (lon % lon_count) * lat_count + lat

    def lat_far(lat, lon):
        if lat == 0:
            return at(0, lon ^ 1)
        if lat == lat_count - 1:
            return at(lat, lon_count - 1 - lon)
        return at(lat + 1 if lat % 2 else lat - 1, lon)

    cells = [(lat, lon) for lat in range(lat_count) for lon in range(lon_count)]
    lon_near = [(at(a, o), at(a, o ^ 1)) for a, o in cells]
    lon_far = [(at(a, o), at(a, o + 1 if o % 2 else o - 1)) for a, o in cells]
    lat_near = [(at(a, o), at(a ^ 1, o)) for a, o in cells]
    return lon_near, lon_far, lat_near, [(at(a, o), lat_far(a, o)) for a, o in cells]


def swap(value, pairs):
    return lax.ppermute(value, ("lon", "lat"), pairs)


def on_device(t, s, u, v, ps, wet):
    lon_near, lon_far, lat_near, lat_far = exchanges(lax.axis_size("lon"), lax.axis_size("lat"))
    inputs = (t, s, u, v, ps, wet)
    cols = jax.ShapeDtypeStruct((COL_ROWS, LANES), jnp.float32)
    rows = jax.ShapeDtypeStruct((ROW_ROWS, LANES), jnp.float32)
    corners = jax.ShapeDtypeStruct((8, LANES), jnp.float32)
    big = pltpu.CompilerParams(vmem_limit_bytes=48 * 1024 * 1024)
    col_near, col_far = pl.pallas_call(
        pack_columns, out_shape=(cols, cols), in_specs=[VMEM] * 6, out_specs=(VMEM, VMEM), compiler_params=big
    )(*inputs)
    row_near, row_far = pl.pallas_call(
        pack_rows, out_shape=(rows, rows), in_specs=[VMEM] * 6, out_specs=(VMEM, VMEM), compiler_params=big
    )(*inputs)
    col_far = swap(col_far, lon_far)
    col_near = swap(col_near, lon_near)
    corner_near, corner_far = pl.pallas_call(
        pack_corners, out_shape=(corners, corners), in_specs=[VMEM] * 2, out_specs=(VMEM, VMEM)
    )(col_near, col_far)
    row_near = lax.dynamic_update_slice(row_near, corner_near, (ROW_CORNER, 0))
    row_far = lax.dynamic_update_slice(row_far, corner_far, (ROW_CORNER, 0))
    row_far = swap(row_far, lat_far)
    row_near = swap(row_near, lat_near)
    out = jax.ShapeDtypeStruct(t.shape, jnp.float32)
    wide = (LEVELS, EXT_ROWS, EXT_LANES)
    return pl.pallas_call(
        step_kernel,
        out_shape=(out,) * 5,
        in_specs=[VMEM] * 10,
        out_specs=(VMEM,) * 5,
        scratch_shapes=[
            pltpu.VMEM((4, *wide), jnp.float32),
            pltpu.VMEM(wide, jnp.float32),
            pltpu.VMEM(wide[1:], jnp.float32),
            pltpu.VMEM(wide, jnp.float32),
            pltpu.VMEM((4, *wide), jnp.float32),
        ],
        compiler_params=big,
    )(*inputs, col_near, col_far, row_near, row_far)


def solution(mesh):
    field = P(None, "lat", "lon")
    return jax.shard_map(
        on_device,
        mesh=mesh,
        in_specs=(field, field, field, field, P("lat", "lon"), field),
        out_specs=(field,) * 5,
        check_vma=False,
    )
```

```python
import jax
import jax.numpy as jnp
from jax import lax
from jax.experimental import pallas as pl
from jax.experimental.pallas import tpu as pltpu
from jax.sharding import PartitionSpec as P

STEPS = 2
HEAT_EXPANSION = 0.2
SALT_CONTRACTION = 0.15
GRAVITY = 0.5
TIME_STEP = 0.2
VISCOSITY = 0.25
DIFFUSIVITY = 0.2
ROTATION = 1.0

LEVELS = 16
ROWS = 32
LANES = 128
BLOCKS = ROWS // 8
SLOTS = LEVELS * BLOCKS

COL_T, COL_S, COL_U, COL_V, COL_WET, COL_PS = range(6)
COL_TILE = 8
COL_ROWS = 6 * COL_TILE
ROW_WET = 4 * 2 * LEVELS
ROW_PS = ROW_WET + LEVELS
ROW_CORNER = ROW_PS + 8
ROW_ROWS = ROW_CORNER + 8

PARTS = 4

VMEM = pl.BlockSpec(memory_space=pltpu.VMEM)
HBM = pl.BlockSpec(memory_space=pltpu.HBM)


def lanes_of(shape):
    return lax.broadcasted_iota(jnp.int32, shape, len(shape) - 1)


def fetch(pairs, sems):
    copies = [pltpu.make_async_copy(src, dst, sems.at[i]) for i, (src, dst) in enumerate(pairs)]
    for copy in copies:
        copy.start()
    return copies


def pack_columns(
    t_hbm, s_hbm, u_hbm, v_hbm, ps_hbm, wet_hbm, near_ref, far_ref,
    t_ref, s_ref, u_ref, v_ref, ps_ref, wet_ref, sems,
):
    copies = fetch(
        (
            (t_hbm, t_ref), (s_hbm, s_ref), (u_hbm, u_ref), (v_hbm, v_ref),
            (wet_hbm, wet_ref), (ps_hbm, ps_ref),
        ),
        sems,
    )
    even = lax.axis_index("lon") % 2 == 0
    slot = lanes_of((8, LANES)) >> 1
    masks = [slot == j for j in range(SLOTS)]

    def pack(index, tiles):
        east = jnp.zeros((8, LANES), jnp.float32)
        west = jnp.zeros((8, LANES), jnp.float32)
        for j, tile in enumerate(tiles):
            rolled = pltpu.roll(tile(), (2 * j + 2) % LANES, 1)
            east = jnp.where(masks[j], rolled, east)
            west = jnp.where(masks[(j + 1) % SLOTS], rolled, west)
        rows = pl.ds(index * COL_TILE, COL_TILE)
        near_ref[rows, :] = jnp.where(even, east, west)
        far_ref[rows, :] = jnp.where(even, west, east)

    def tiles_of(ref):
        return [
            (lambda j=j: ref[j // BLOCKS, pl.ds(8 * (j % BLOCKS), 8), :].astype(jnp.float32))
            for j in range(SLOTS)
        ]

    for index, ref in ((COL_T, t_ref), (COL_S, s_ref), (COL_U, u_ref), (COL_V, v_ref), (COL_WET, wet_ref)):
        copies[index].wait()
        pack(index, tiles_of(ref))
    copies[COL_PS].wait()
    pack(COL_PS, [(lambda r=r: ps_ref[pl.ds(8 * r, 8), :]) for r in range(BLOCKS)])


def reverse_lanes(value):
    index = LANES - 1 - lanes_of(value.shape)
    return jnp.take_along_axis(value, index, axis=1, mode="promise_in_bounds")


def pack_rows(
    t_hbm, s_hbm, u_hbm, v_hbm, ps_hbm, wet_hbm, near_ref, far_ref, x_ref, wet_ref, ps_ref, sems
):
    pairs = [(ps_hbm, ps_ref)]
    for side, first in ((0, 0), (1, ROWS - 8)):
        for index, src in enumerate((t_hbm, s_hbm, u_hbm, v_hbm)):
            pairs.append((src.at[:, pl.ds(first, 8), :], x_ref.at[side, index]))
        pairs.append((wet_hbm.at[:, pl.ds(first, 8), :], wet_ref.at[side]))
    copies = fetch(pairs, sems)
    lat = lax.axis_index("lat")
    even = lat % 2 == 0
    fold = lat == lax.axis_size("lat") - 1
    for copy in copies:
        copy.wait()

    def put(first, north, south, sign):
        rows = pl.ds(first, north.shape[0])
        near_ref[rows, :] = jnp.where(even, north, south)
        far_ref[rows, :] = jnp.where(even, south, north)

        @pl.when(fold)
        def _():
            far_ref[rows, :] = sign * reverse_lanes(north)

    for index, sign in enumerate((1.0, 1.0, -1.0, -1.0)):
        for ring in range(2):
            put((2 * index + ring) * LEVELS, x_ref[1, index, :, 7 - ring, :], x_ref[0, index, :, ring, :], sign)
    put(ROW_WET, wet_ref[1, :, 7, :].astype(jnp.float32), wet_ref[0, :, 0, :].astype(jnp.float32), 1.0)
    top, bottom = ps_ref[pl.ds(ROWS - 8, 8), :], ps_ref[pl.ds(0, 8), :]
    sub = lax.broadcasted_iota(jnp.int32, (8, LANES), 0)
    north = jnp.where(sub == 0, pltpu.roll(top, 1, 0), pltpu.roll(top, 3, 0))
    put(ROW_PS, north, bottom, 1.0)
    near_ref[pl.ds(ROW_CORNER, 8), :] = jnp.zeros((8, LANES), jnp.float32)
    far_ref[pl.ds(ROW_CORNER, 8), :] = jnp.zeros((8, LANES), jnp.float32)


def halo_tiles(near, far, even_lon):
    slot = lanes_of(near.shape) >> 1
    west = jnp.where(even_lon, far, near)
    east = jnp.where(even_lon, near, far)
    return (
        jnp.where(slot % 2 == 0, west, east),
        jnp.where(slot % 2 == 0, east, west),
    )


def pack_corners(far_ref, near_ref, far_in, near_in, far_out, near_out):
    lat = lax.axis_index("lat")
    even = lat % 2 == 0
    fold = lat == lax.axis_size("lat") - 1
    even_tile, odd_tile = halo_tiles(near_ref[...], far_ref[...], lax.axis_index("lon") % 2 == 0)
    lane = lanes_of((8, LANES))
    sub = lax.broadcasted_iota(jnp.int32, (8, LANES), 0)

    def gather(tile, row):
        out = jnp.zeros((8, LANES), jnp.float32)
        for index, field in enumerate((COL_T, COL_S, COL_U, COL_V, COL_PS)):
            one = pltpu.roll(tile[field * COL_TILE : (field + 1) * COL_TILE], (index - row) % 8, 0)
            out = jnp.where(sub == index, one, out)
        return out

    north, south = gather(odd_tile, 7), gather(even_tile, 0)
    mirrored = pltpu.roll(north, LANES - 6, 1)
    mirrored = jnp.where(lane % 2 == 0, pltpu.roll(mirrored, 1, 1), pltpu.roll(mirrored, LANES - 1, 1))
    mirrored = jnp.where((sub == 2) | (sub == 3), -mirrored, mirrored)
    rows = pl.ds(ROW_CORNER, 8)
    near_out[rows, :] = jnp.where(even, north, south)
    far_out[rows, :] = jnp.where(fold, mirrored, jnp.where(even, south, north))


def laplace(q):
    centre, east, west, north, south = q
    return east + west + north + south - 4.0 * centre


def march(t, s, u, v, p, wet, coriolis):
    grad_x = 0.5 * (p[1] - p[2])
    grad_y = 0.5 * (p[3] - p[4])

    def tracer(q):
        transport = -0.5 * (u[0] * (q[1] - q[2]) + v[0] * (q[3] - q[4]))
        return wet * (q[0] + TIME_STEP * (transport + DIFFUSIVITY * laplace(q)))

    return (
        tracer(t),
        tracer(s),
        wet * (u[0] + TIME_STEP * (coriolis * v[0] - grad_x + VISCOSITY * laplace(u))),
        wet * (v[0] + TIME_STEP * (-coriolis * u[0] - grad_y + VISCOSITY * laplace(v))),
    )


def heaviness(t, s):
    return -HEAT_EXPANSION * t + SALT_CONTRACTION * s


def coriolis_of(row):
    total = ROWS * lax.axis_size("lat")
    row = jnp.minimum(lax.axis_index("lat") * ROWS + row, total - 1).astype(jnp.float32)
    return ROTATION * (2.0 * (row + 0.5) / total - 1.0)


def east_of(own, halo, lane):
    return pltpu.roll(jnp.where(lane == 0, halo, own), LANES - 1, 1)


def west_of(own, halo, lane):
    return pltpu.roll(jnp.where(lane == LANES - 1, halo, own), 1, 1)


def packed_pressure(t, s, ps, order):
    heavy = heaviness(t, s)
    total = heavy
    for shift in (8, 16, 32, 64):
        total = total + jnp.where(order >= shift, pltpu.roll(total, shift, 1), 0.0)
        ps = ps + pltpu.roll(ps, shift, 1)
    return ps + GRAVITY * (total - 0.5 * heavy)


def main_kernel(
    t_ref, s_ref, u_ref, v_ref, ps_ref, wet_ref, near_ref, far_ref, own_near_ref, own_far_ref,
    t_hbm, s_hbm, u_hbm, v_hbm, p_hbm, raw_ref, rawh_ref, one_ref, oneh_ref, psh_ref,
    p_ref, y_ref, q_ref, out_ref, sems,
):
    even = lax.axis_index("lon") % 2 == 0
    near, far = near_ref[...], far_ref[...]
    own_near, own_far = own_near_ref[...], own_far_ref[...]
    own_east, own_west = jnp.where(even, own_near, own_far), jnp.where(even, own_far, own_near)
    got_west, got_east = jnp.where(even, far, near), jnp.where(even, near, far)
    odd = lanes_of(near.shape) % 2 == 1
    even_tile, odd_tile = halo_tiles(near, far, even)

    z = jnp.where(odd, got_west, got_east)
    z_east = pltpu.roll(jnp.where(odd, got_east, own_west), LANES - 1, 1)
    z_west = pltpu.roll(jnp.where(odd, own_east, got_west), 1, 1)
    lane = lanes_of((8, LANES))
    sub = lax.broadcasted_iota(jnp.int32, (8, LANES), 0)
    order = (lane + LANES - 1) % LANES

    def tile(value, index):
        return value[index * COL_TILE : (index + 1) * COL_TILE]

    def above(q):
        return jnp.where(sub == 7, pltpu.roll(pltpu.roll(q, LANES - 2, 1), 7, 0), pltpu.roll(q, 7, 0))

    def below(q):
        return jnp.where(sub == 0, pltpu.roll(pltpu.roll(q, 2, 1), 1, 0), pltpu.roll(q, 1, 0))

    zp, zp_east, zp_west = (
        packed_pressure(tile(q, COL_T), tile(q, COL_S), tile(q, COL_PS), order) for q in (z, z_east, z_west)
    )

    def around(index):
        q = tile(z, index)
        return q, tile(z_east, index), tile(z_west, index), above(q), below(q)

    z_one = march(
        around(COL_T), around(COL_S), around(COL_U), around(COL_V),
        (zp, zp_east, zp_west, above(zp), below(zp)),
        tile(z, COL_WET),
        coriolis_of(8 * ((order // 2) % BLOCKS) + sub),
    )
    zp_one = packed_pressure(z_one[0], z_one[1], tile(z, COL_PS), order)

    for side, block, tiles in ((0, 0, even_tile), (1, BLOCKS - 1, odd_tile)):
        psh_ref[side] = pltpu.roll(tile(tiles, COL_PS), LANES - 2 * (block + 1), 1)

    fields = (t_ref, s_ref, u_ref, v_ref)
    outs = (t_hbm, s_hbm, u_hbm, v_hbm, p_hbm)
    blocks = [pl.ds(8 * r, 8) for r in range(BLOCKS)]
    coriolis = [coriolis_of(8 * r + sub) for r in range(BLOCKS)]
    psv = [ps_ref[rows, :] for rows in blocks]

    def vertical(ref, lead, r, centre):
        north = ref[(*lead, pl.ds(8 * r + 1, 8))] if r < BLOCKS - 1 else pltpu.roll(centre, 7, 0)
        south = ref[(*lead, pl.ds(8 * r - 1, 8))] if r > 0 else pltpu.roll(centre, 1, 0)
        return north, south

    def level(k, running):
        run0, run1, run2 = (list(x) for x in running)
        side_of = {0: 0, BLOCKS - 1: 1}
        shifts = [LANES - 2 - 8 * k - 2 * r for r in range(BLOCKS)]
        for r, rows in enumerate(blocks):
            heavy = heaviness(t_ref[k, rows, :], s_ref[k, rows, :])
            p_ref[rows, :] = psv[r] + GRAVITY * (run0[r] + 0.5 * heavy)
            run0[r] = run0[r] + heavy
        for r, rows in enumerate(blocks):
            tiles = odd_tile if r % 2 else even_tile
            side = side_of.get(r)

            def parts(index, ref):
                own = ref[k, rows, :]
                halo = pltpu.roll(tile(tiles, index), shifts[r], 1)
                if side is not None:
                    raw_ref[side, index, k] = own
                    rawh_ref[side, index, k] = halo
                return (own, east_of(own, halo, lane), west_of(own, halo, lane), *vertical(ref, (k,), r, own))

            own = p_ref[rows, :]
            halo = pltpu.roll(zp, shifts[r], 1)
            p = (own, east_of(own, halo, lane), west_of(own, halo, lane), *vertical(p_ref, (), r, own))
            wet = wet_ref[k, rows, :].astype(jnp.float32)
            if side is not None:
                raw_ref[side, 4, k] = wet
                rawh_ref[side, 4, k] = pltpu.roll(tile(tiles, COL_WET), shifts[r], 1)
            new = march(*(parts(i, ref) for i, ref in enumerate(fields)), p, wet, coriolis[r])
            for index in range(4):
                y_ref[index, rows, :] = new[index]
            heavy = heaviness(new[0], new[1])
            q_ref[rows, :] = psv[r] + GRAVITY * (run1[r] + 0.5 * heavy)
            run1[r] = run1[r] + heavy
        for r, rows in enumerate(blocks):
            side = side_of.get(r)

            def parts(index):
                own = y_ref[index, rows, :]
                halo = pltpu.roll(z_one[index], shifts[r], 1)
                if side is not None:
                    one_ref[side, index, k] = own
                    oneh_ref[side, index, k] = halo
                return (own, east_of(own, halo, lane), west_of(own, halo, lane), *vertical(y_ref, (index,), r, own))

            own = q_ref[rows, :]
            halo = pltpu.roll(zp_one, shifts[r], 1)
            p = (own, east_of(own, halo, lane), west_of(own, halo, lane), *vertical(q_ref, (), r, own))
            wet = wet_ref[k, rows, :].astype(jnp.float32)
            new = march(*(parts(i) for i in range(4)), p, wet, coriolis[r])
            for index in range(4):
                out_ref[index, k, rows, :] = new[index]
            heavy = heaviness(new[0], new[1])
            out_ref[4, k, rows, :] = psv[r] + GRAVITY * (run2[r] + 0.5 * heavy)
            run2[r] = run2[r] + heavy
        return tuple(tuple(x) for x in (run0, run1, run2))

    zero = tuple(jnp.zeros((8, LANES), jnp.float32) for _ in range(BLOCKS))
    running = (zero, zero, zero)
    copies = []
    for part in range(PARTS):
        levels = pl.ds(part * LEVELS // PARTS, LEVELS // PARTS)
        running = lax.fori_loop(part * LEVELS // PARTS, (part + 1) * LEVELS // PARTS, level, running)
        for index, out in enumerate(outs):
            copy = pltpu.make_async_copy(out_ref.at[index, levels], out.at[levels], sems.at[part, index])
            copy.start()
            copies.append(copy)
    for copy in copies:
        copy.wait()


def patch_kernel(
    ps_ref, far_ref, near_ref, raw_ref, rawh_ref, one_ref, oneh_ref, psh_ref, t_in, s_in, u_in, v_in, p_in,
    t_hbm, s_hbm, u_hbm, v_hbm, p_hbm, block_ref, in_sems, out_sems,
):
    outs = (t_hbm, s_hbm, u_hbm, v_hbm, p_hbm)
    firsts = (0, ROWS - 8)
    loads = [
        [
            pltpu.make_async_copy(out.at[:, pl.ds(first, 8), :], block_ref.at[side, index], in_sems.at[side, index])
            for index, out in enumerate(outs)
        ]
        for side, first in enumerate(firsts)
    ]
    stores = [
        [
            pltpu.make_async_copy(block_ref.at[side, index], out.at[:, pl.ds(first, 8), :], out_sems.at[side, index])
            for index, out in enumerate(outs)
        ]
        for side, first in enumerate(firsts)
    ]
    for copy in loads[0] + loads[1]:
        copy.start()
    lat = lax.axis_index("lat")
    even = lat % 2 == 0
    lane = lanes_of((LEVELS, LANES))
    depth = lax.broadcasted_iota(jnp.int32, (LEVELS, LANES), 0)
    near, far = near_ref[...], far_ref[...]
    south = jnp.where(lat == 0, 0.0, jnp.where(even, far, near))
    north = jnp.where(even, near, far)

    def pressure(t, s, ps):
        heavy = heaviness(t, s)
        total = heavy
        for shift in (1, 2, 4, 8):
            total = total + jnp.where(depth >= shift, pltpu.roll(total, shift, 0), 0.0)
        return ps + GRAVITY * (total - 0.5 * heavy)

    def side_rows(side, value):
        rows = (0, 1, 2) if side == 0 else (7, 6, 5)
        at = [firsts[side] + r for r in rows]
        block = BLOCKS - 1 if side == 0 else 0

        def unfold(row):
            row = jnp.broadcast_to(pltpu.roll(row, LANES - 2 * (block + 1), 1), (LEVELS, LANES))
            for bit in (1, 2, 4, 8):
                row = jnp.where(depth & bit != 0, pltpu.roll(row, LANES - 8 * bit, 1), row)
            return row

        def five(own, halo, out, inn):
            ns = (inn, out) if side == 0 else (out, inn)
            return (own, east_of(own, halo, lane), west_of(own, halo, lane), *ns)

        def five_halo(own, halo, out, inn):
            ns = (inn, out) if side == 0 else (out, inn)
            return (halo, east_of(halo, own, lane), west_of(halo, own, lane), *ns)

        ring2 = [value[(2 * i + 1) * LEVELS : (2 * i + 2) * LEVELS] for i in range(4)]
        ring1 = [value[2 * i * LEVELS : (2 * i + 1) * LEVELS] for i in range(4)]
        corner = [unfold(value[ROW_CORNER + i : ROW_CORNER + i + 1]) for i in range(5)]
        edge0 = [raw_ref[side, i, :, rows[0], :] for i in range(5)]
        edge0h = [rawh_ref[side, i, :, rows[0], :] for i in range(5)]
        edge1 = [raw_ref[side, i, :, rows[1], :] for i in range(5)]
        edge1h = [rawh_ref[side, i, :, rows[1], :] for i in range(4)]
        one1 = [one_ref[side, i, :, rows[1], :] for i in range(4)]
        one1h = [oneh_ref[side, i, :, rows[1], :] for i in range(4)]
        one2 = [one_ref[side, i, :, rows[2], :] for i in range(4)]
        wet_ring = value[ROW_WET : ROW_WET + LEVELS]
        ps_ring2, ps_ring1 = value[ROW_PS + 1 : ROW_PS + 2], value[ROW_PS : ROW_PS + 1]
        ps_corner = corner[4][0:1]
        ps0, ps1, ps2 = (ps_ref[pl.ds(a, 1), :] for a in at)
        ps0h, ps1h = (psh_ref[side, pl.ds(r, 1), :] for r in rows[:2])
        step = -1 if side == 0 else 1
        cor_ring, cor0, cor1 = (coriolis_of(jnp.int32(at[0] + d)) for d in (step, 0, -step))

        p_ring2 = pressure(ring2[0], ring2[1], ps_ring2)
        p_ring1 = pressure(ring1[0], ring1[1], ps_ring1)
        p_corner = pressure(corner[0], corner[1], ps_corner)
        p0 = pressure(edge0[0], edge0[1], ps0)
        p0h = pressure(edge0h[0], edge0h[1], ps0h)
        p1 = pressure(edge1[0], edge1[1], ps1)
        p1h = pressure(edge1h[0], edge1h[1], ps1h)
        first_ring = march(
            *(five(ring1[i], corner[i], ring2[i], edge0[i]) for i in range(4)),
            five(p_ring1, p_corner, p_ring2, p0), wet_ring, cor_ring,
        )
        first0 = march(
            *(five(edge0[i], edge0h[i], ring1[i], edge1[i]) for i in range(4)),
            five(p0, p0h, p_ring1, p1), edge0[4], cor0,
        )
        first0h = march(
            *(five_halo(edge0[i], edge0h[i], corner[i], edge1h[i]) for i in range(4)),
            five_halo(p0, p0h, p_corner, p1h), edge0h[4], cor0,
        )
        p_ring1 = pressure(first_ring[0], first_ring[1], ps_ring1)
        p0 = pressure(first0[0], first0[1], ps0)
        p0h = pressure(first0h[0], first0h[1], ps0h)
        p1 = pressure(one1[0], one1[1], ps1)
        p1h = pressure(one1h[0], one1h[1], ps1h)
        p2 = pressure(one2[0], one2[1], ps2)
        second0 = march(
            *(five(first0[i], first0h[i], first_ring[i], one1[i]) for i in range(4)),
            five(p0, p0h, p_ring1, p1), edge0[4], cor0,
        )
        second1 = march(
            *(five(one1[i], one1h[i], first0[i], one2[i]) for i in range(4)),
            five(p1, p1h, p0, p2), edge1[4], cor1,
        )
        second0 = (*second0, pressure(second0[0], second0[1], ps0))
        second1 = (*second1, pressure(second1[0], second1[1], ps1))
        for index in range(5):
            loads[side][index].wait()
            block_ref[side, index, :, rows[0], :] = second0[index]
            block_ref[side, index, :, rows[1], :] = second1[index]
            stores[side][index].start()

    side_rows(0, south)
    side_rows(1, north)
    for copy in stores[0] + stores[1]:
        copy.wait()


def exchanges(lon_count, lat_count):
    def at(lat, lon):
        return (lon % lon_count) * lat_count + lat

    def lat_far(lat, lon):
        if lat == 0:
            return at(0, lon ^ 1)
        if lat == lat_count - 1:
            return at(lat, lon_count - 1 - lon)
        return at(lat + 1 if lat % 2 else lat - 1, lon)

    cells = [(lat, lon) for lat in range(lat_count) for lon in range(lon_count)]
    lon_near = [(at(a, o), at(a, o ^ 1)) for a, o in cells]
    lon_far = [(at(a, o), at(a, o + 1 if o % 2 else o - 1)) for a, o in cells]
    lat_near = [(at(a, o), at(a ^ 1, o)) for a, o in cells]
    return lon_near, lon_far, lat_near, [(at(a, o), lat_far(a, o)) for a, o in cells]


def swap(value, pairs):
    return lax.ppermute(value, ("lon", "lat"), pairs)


def on_device(t, s, u, v, ps, wet):
    lon_near, lon_far, lat_near, lat_far = exchanges(lax.axis_size("lon"), lax.axis_size("lat"))
    inputs = (t, s, u, v, ps, wet)
    kept = [pltpu.with_memory_space_constraint(x, pltpu.HBM) for x in inputs]
    cols = jax.ShapeDtypeStruct((COL_ROWS, LANES), jnp.float32)
    rows = jax.ShapeDtypeStruct((ROW_ROWS, LANES), jnp.float32)

    def grant(mib):
        return pltpu.CompilerParams(vmem_limit_bytes=int(mib * 1024 * 1024))

    col_near, col_far = pl.pallas_call(
        pack_columns,
        out_shape=(cols, cols),
        in_specs=[HBM] * 6,
        out_specs=(VMEM, VMEM),
        scratch_shapes=[pltpu.VMEM(x.shape, x.dtype) for x in inputs] + [pltpu.SemaphoreType.DMA((6,))],
        compiler_params=grant(6),
    )(*kept)
    block = (LEVELS, 8, LANES)
    row_near, row_far = pl.pallas_call(
        pack_rows,
        out_shape=(rows, rows),
        in_specs=[HBM] * 6,
        out_specs=(VMEM, VMEM),
        scratch_shapes=[
            pltpu.VMEM((2, 4, *block), jnp.float32),
            pltpu.VMEM((2, *block), jnp.int32),
            pltpu.VMEM((ROWS, LANES), jnp.float32),
            pltpu.SemaphoreType.DMA((11,)),
        ],
        compiler_params=grant(4),
    )(*kept)
    got_far = swap(col_far, lon_far)
    got_near = swap(col_near, lon_near)
    row_far, row_near = pl.pallas_call(
        pack_corners,
        out_shape=(rows, rows),
        in_specs=[VMEM] * 4,
        out_specs=(VMEM, VMEM),
        input_output_aliases={2: 0, 3: 1},
        compiler_params=grant(2),
    )(got_far, got_near, row_far, row_near)
    row_far = swap(row_far, lat_far)
    row_near = swap(row_near, lat_near)
    out = jax.ShapeDtypeStruct(t.shape, jnp.float32)

    def blocks(count):
        return jax.ShapeDtypeStruct((2, count, *block), jnp.float32)

    plane = pltpu.VMEM((ROWS, LANES), jnp.float32)
    *outs, raw, raw_halo, one, one_halo, ps_halo = pl.pallas_call(
        main_kernel,
        out_shape=(out,) * 5 + (blocks(5), blocks(5), blocks(4), blocks(4), jax.ShapeDtypeStruct((2, 8, LANES), jnp.float32)),
        in_specs=[VMEM] * 10,
        out_specs=(HBM,) * 5 + (VMEM,) * 5,
        scratch_shapes=[
            plane,
            pltpu.VMEM((4, ROWS, LANES), jnp.float32),
            plane,
            pltpu.VMEM((5, *t.shape), jnp.float32),
            pltpu.SemaphoreType.DMA((PARTS, 5)),
        ],
        compiler_params=grant(12),
    )(*inputs, got_near, got_far, col_near, col_far)
    return pl.pallas_call(
        patch_kernel,
        out_shape=(out,) * 5,
        in_specs=[VMEM] * 8 + [HBM] * 5,
        out_specs=(HBM,) * 5,
        scratch_shapes=[
            pltpu.VMEM((2, 5, *block), jnp.float32),
            pltpu.SemaphoreType.DMA((2, 5)),
            pltpu.SemaphoreType.DMA((2, 5)),
        ],
        input_output_aliases={8 + i: i for i in range(5)},
        compiler_params=grant(8),
    )(ps, row_far, row_near, raw, raw_halo, one, one_halo, ps_halo, *outs)


def solution(mesh):
    field = P(None, "lat", "lon")
    return jax.shard_map(
        on_device,
        mesh=mesh,
        in_specs=(field, field, field, field, P("lat", "lon"), field),
        out_specs=(field,) * 5,
        check_vma=False,
    )
```

```python
import jax
import jax.numpy as jnp
from jax import lax
from jax.experimental import pallas as pl
from jax.experimental.pallas import tpu as pltpu
from jax.sharding import PartitionSpec as P

STEPS = 2
HEAT_EXPANSION = 0.2
SALT_CONTRACTION = 0.15
GRAVITY = 0.5
TIME_STEP = 0.2
VISCOSITY = 0.25
DIFFUSIVITY = 0.2
ROTATION = 1.0

LEVELS = 16
ROWS = 32
LANES = 128
BLOCKS = ROWS // 8
SLOTS = LEVELS * BLOCKS

COL_T, COL_S, COL_U, COL_V, COL_WET, COL_PS = range(6)
COL_TILE = 8
COL_ROWS = 6 * COL_TILE
ROW_WET = 4 * 2 * LEVELS
ROW_PS = ROW_WET + LEVELS
ROW_CORNER = ROW_PS + 8
ROW_ROWS = ROW_CORNER + 8

PARTS = 4

VMEM = pl.BlockSpec(memory_space=pltpu.VMEM)
HBM = pl.BlockSpec(memory_space=pltpu.HBM)


def lanes_of(shape):
    return lax.broadcasted_iota(jnp.int32, shape, len(shape) - 1)


def pack_columns(
    t_hbm, s_hbm, u_hbm, v_hbm, ps_hbm, wet_hbm, near_ref, far_ref, x_ref, wet_ref, ps_ref, sems
):
    for index, src in enumerate((t_hbm, s_hbm, u_hbm, v_hbm)):
        pltpu.make_async_copy(src, x_ref.at[index], sems.at[0]).start()
    rest = (
        pltpu.make_async_copy(wet_hbm, wet_ref, sems.at[1]),
        pltpu.make_async_copy(ps_hbm, ps_ref, sems.at[2]),
    )
    for copy in rest:
        copy.start()
    even = lax.axis_index("lon") % 2 == 0
    slot = lanes_of((8, LANES)) >> 1
    masks = [slot == j for j in range(SLOTS)]

    def pack(index, tiles):
        east = jnp.zeros((8, LANES), jnp.float32)
        west = jnp.zeros((8, LANES), jnp.float32)
        for j, tile in enumerate(tiles):
            rolled = pltpu.roll(tile(), (2 * j + 2) % LANES, 1)
            east = jnp.where(masks[j], rolled, east)
            west = jnp.where(masks[(j + 1) % SLOTS], rolled, west)
        rows = pl.ds(index * COL_TILE, COL_TILE)
        near_ref[rows, :] = jnp.where(even, east, west)
        far_ref[rows, :] = jnp.where(even, west, east)

    def tiles_of(ref):
        return [
            (lambda j=j: ref[j // BLOCKS, pl.ds(8 * (j % BLOCKS), 8), :].astype(jnp.float32))
            for j in range(SLOTS)
        ]

    pltpu.make_async_copy(x_ref, x_ref, sems.at[0]).wait()
    for index in range(4):
        pack(index, tiles_of(x_ref.at[index]))
    for copy in rest:
        copy.wait()
    pack(COL_WET, tiles_of(wet_ref))
    pack(COL_PS, [(lambda r=r: ps_ref[pl.ds(8 * r, 8), :]) for r in range(BLOCKS)])


def reverse_lanes(value):
    index = LANES - 1 - lanes_of(value.shape)
    return jnp.take_along_axis(value, index, axis=1, mode="promise_in_bounds")


def pack_rows(
    t_hbm, s_hbm, u_hbm, v_hbm, ps_hbm, wet_hbm, near_ref, far_ref, x_ref, wet_ref, ps_ref, sems
):
    rest = pltpu.make_async_copy(ps_hbm, ps_ref, sems.at[2])
    rest.start()
    for side, first in ((0, 0), (1, ROWS - 8)):
        for index, src in enumerate((t_hbm, s_hbm, u_hbm, v_hbm)):
            pltpu.make_async_copy(src.at[:, pl.ds(first, 8), :], x_ref.at[side, index], sems.at[0]).start()
        pltpu.make_async_copy(wet_hbm.at[:, pl.ds(first, 8), :], wet_ref.at[side], sems.at[1]).start()
    lat = lax.axis_index("lat")
    even = lat % 2 == 0
    fold = lat == lax.axis_size("lat") - 1
    for ref, sem in ((x_ref, 0), (wet_ref, 1)):
        pltpu.make_async_copy(ref, ref, sems.at[sem]).wait()
    rest.wait()

    def put(first, north, south, sign):
        rows = pl.ds(first, north.shape[0])
        near_ref[rows, :] = jnp.where(even, north, south)
        far_ref[rows, :] = jnp.where(even, south, north)

        @pl.when(fold)
        def _():
            far_ref[rows, :] = sign * reverse_lanes(north)

    for index, sign in enumerate((1.0, 1.0, -1.0, -1.0)):
        for ring in range(2):
            put((2 * index + ring) * LEVELS, x_ref[1, index, :, 7 - ring, :], x_ref[0, index, :, ring, :], sign)
    put(ROW_WET, wet_ref[1, :, 7, :].astype(jnp.float32), wet_ref[0, :, 0, :].astype(jnp.float32), 1.0)
    top, bottom = ps_ref[pl.ds(ROWS - 8, 8), :], ps_ref[pl.ds(0, 8), :]
    sub = lax.broadcasted_iota(jnp.int32, (8, LANES), 0)
    north = jnp.where(sub == 0, pltpu.roll(top, 1, 0), pltpu.roll(top, 3, 0))
    put(ROW_PS, north, bottom, 1.0)
    near_ref[pl.ds(ROW_CORNER, 8), :] = jnp.zeros((8, LANES), jnp.float32)
    far_ref[pl.ds(ROW_CORNER, 8), :] = jnp.zeros((8, LANES), jnp.float32)


def halo_tiles(near, far, even_lon):
    slot = lanes_of(near.shape) >> 1
    west = jnp.where(even_lon, far, near)
    east = jnp.where(even_lon, near, far)
    return (
        jnp.where(slot % 2 == 0, west, east),
        jnp.where(slot % 2 == 0, east, west),
    )


def pack_corners(far_ref, near_ref, far_in, near_in, far_out, near_out):
    lat = lax.axis_index("lat")
    even = lat % 2 == 0
    fold = lat == lax.axis_size("lat") - 1
    even_tile, odd_tile = halo_tiles(near_ref[...], far_ref[...], lax.axis_index("lon") % 2 == 0)
    lane = lanes_of((8, LANES))
    sub = lax.broadcasted_iota(jnp.int32, (8, LANES), 0)

    def gather(tile, row):
        out = jnp.zeros((8, LANES), jnp.float32)
        for index, field in enumerate((COL_T, COL_S, COL_U, COL_V, COL_PS)):
            one = pltpu.roll(tile[field * COL_TILE : (field + 1) * COL_TILE], (index - row) % 8, 0)
            out = jnp.where(sub == index, one, out)
        return out

    north, south = gather(odd_tile, 7), gather(even_tile, 0)
    mirrored = pltpu.roll(north, LANES - 6, 1)
    mirrored = jnp.where(lane % 2 == 0, pltpu.roll(mirrored, 1, 1), pltpu.roll(mirrored, LANES - 1, 1))
    mirrored = jnp.where((sub == 2) | (sub == 3), -mirrored, mirrored)
    rows = pl.ds(ROW_CORNER, 8)
    near_out[rows, :] = jnp.where(even, north, south)
    far_out[rows, :] = jnp.where(fold, mirrored, jnp.where(even, south, north))


def laplace(q):
    centre, east, west, north, south = q
    return east + west + north + south - 4.0 * centre


def slopes(u, p):
    return VISCOSITY * u - 0.5 * p, VISCOSITY * u + 0.5 * p


def march(t, s, u, v, p, sides, wet, coriolis):
    grad_y = 0.5 * (p[0] - p[1])

    def tracer(q):
        transport = -0.5 * (u[0] * (q[1] - q[2]) + v[0] * (q[3] - q[4]))
        return wet * (q[0] + TIME_STEP * (transport + DIFFUSIVITY * laplace(q)))

    push = sides[0] + sides[1] + VISCOSITY * (u[1] + u[2]) - 4.0 * VISCOSITY * u[0]
    return (
        tracer(t),
        tracer(s),
        wet * (u[0] + TIME_STEP * (coriolis * v[0] + push)),
        wet * (v[0] + TIME_STEP * (-coriolis * u[0] - grad_y + VISCOSITY * laplace(v))),
    )


def heaviness(t, s):
    return -HEAT_EXPANSION * t + SALT_CONTRACTION * s


def coriolis_of(row):
    total = ROWS * lax.axis_size("lat")
    row = jnp.minimum(lax.axis_index("lat") * ROWS + row, total - 1).astype(jnp.float32)
    return ROTATION * (2.0 * (row + 0.5) / total - 1.0)


def east_of(own, halo, lane):
    return pltpu.roll(jnp.where(lane == 0, halo, own), LANES - 1, 1)


def west_of(own, halo, lane):
    return pltpu.roll(jnp.where(lane == LANES - 1, halo, own), 1, 1)


def packed_pressure(t, s, ps, order):
    heavy = heaviness(t, s)
    total = heavy
    for shift in (8, 16, 32, 64):
        total = total + jnp.where(order >= shift, pltpu.roll(total, shift, 1), 0.0)
        ps = ps + pltpu.roll(ps, shift, 1)
    return ps + GRAVITY * (total - 0.5 * heavy)


def main_kernel(
    t_ref, s_ref, u_ref, v_ref, ps_ref, wet_ref, near_ref, far_ref, own_near_ref, own_far_ref,
    t_hbm, s_hbm, u_hbm, v_hbm, p_hbm, raw_ref, rawh_ref, one_ref, oneh_ref, psh_ref,
    p_ref, y_ref, q_ref, out_ref, sems,
):
    even = lax.axis_index("lon") % 2 == 0
    near, far = near_ref[...], far_ref[...]
    own_near, own_far = own_near_ref[...], own_far_ref[...]
    own_east, own_west = jnp.where(even, own_near, own_far), jnp.where(even, own_far, own_near)
    got_west, got_east = jnp.where(even, far, near), jnp.where(even, near, far)
    odd = lanes_of(near.shape) % 2 == 1
    even_tile, odd_tile = halo_tiles(near, far, even)

    z = jnp.where(odd, got_west, got_east)
    z_east = pltpu.roll(jnp.where(odd, got_east, own_west), LANES - 1, 1)
    z_west = pltpu.roll(jnp.where(odd, own_east, got_west), 1, 1)
    lane = lanes_of((8, LANES))
    sub = lax.broadcasted_iota(jnp.int32, (8, LANES), 0)
    order = (lane + LANES - 1) % LANES

    def tile(value, index):
        return value[index * COL_TILE : (index + 1) * COL_TILE]

    def above(q):
        return jnp.where(sub == 7, pltpu.roll(pltpu.roll(q, LANES - 2, 1), 7, 0), pltpu.roll(q, 7, 0))

    def below(q):
        return jnp.where(sub == 0, pltpu.roll(pltpu.roll(q, 2, 1), 1, 0), pltpu.roll(q, 1, 0))

    zp, zp_east, zp_west = (
        packed_pressure(tile(q, COL_T), tile(q, COL_S), tile(q, COL_PS), order) for q in (z, z_east, z_west)
    )

    def centred(q):
        return q, above(q), below(q)

    def around(index):
        q = tile(z, index)
        return q, tile(z_east, index), tile(z_west, index), above(q), below(q)

    z_one = march(
        around(COL_T), around(COL_S), centred(tile(z, COL_U)), around(COL_V),
        (above(zp), below(zp)),
        (slopes(tile(z_east, COL_U), zp_east)[0], slopes(tile(z_west, COL_U), zp_west)[1]),
        tile(z, COL_WET),
        coriolis_of(8 * ((order // 2) % BLOCKS) + sub),
    )
    zp_one = packed_pressure(z_one[0], z_one[1], tile(z, COL_PS), order)

    def packed_slopes(u, p):
        to_west, to_east = slopes(u, p)
        return jnp.where(lane % 2 == 1, to_east, to_west)

    z_slopes = packed_slopes(tile(z, COL_U), zp)
    z_one_slopes = packed_slopes(z_one[2], zp_one)

    for side, block, tiles in ((0, 0, even_tile), (1, BLOCKS - 1, odd_tile)):
        psh_ref[side] = pltpu.roll(tile(tiles, COL_PS), LANES - 2 * (block + 1), 1)

    outs = (t_hbm, s_hbm, u_hbm, v_hbm, p_hbm)
    blocks = [pl.ds(8 * r, 8) for r in range(BLOCKS)]
    coriolis = [coriolis_of(8 * r + sub) for r in range(BLOCKS)]
    psv = [ps_ref[rows, :] for rows in blocks]

    def vertical(ref, lead, r, centre):
        north = ref[(*lead, pl.ds(8 * r + 1, 8))] if r < BLOCKS - 1 else pltpu.roll(centre, 7, 0)
        south = ref[(*lead, pl.ds(8 * r - 1, 8))] if r > 0 else pltpu.roll(centre, 1, 0)
        return north, south

    def level(k, running):
        run0, run1, run2 = (list(x) for x in running)
        side_of = {0: 0, BLOCKS - 1: 1}
        shifts = [LANES - 2 - 8 * k - 2 * r for r in range(BLOCKS)]
        for r, rows in enumerate(blocks):
            heavy = heaviness(t_ref[k, rows, :], s_ref[k, rows, :])
            p_ref[rows, :] = psv[r] + GRAVITY * (run0[r] + 0.5 * heavy)
            run0[r] = run0[r] + heavy
        for r, rows in enumerate(blocks):
            tiles = odd_tile if r % 2 else even_tile
            side = side_of.get(r)

            def unpack(index):
                return pltpu.roll(tile(tiles, index), shifts[r], 1)

            def parts(index, ref):
                own, halo = ref[k, rows, :], unpack(index)
                if side is not None:
                    raw_ref[side, index, k] = own
                    rawh_ref[side, index, k] = halo
                return (own, east_of(own, halo, lane), west_of(own, halo, lane), *vertical(ref, (k,), r, own))

            p, u = p_ref[rows, :], u_ref[k, rows, :]
            halo = pltpu.roll(z_slopes, shifts[r], 1)
            to_west, to_east = slopes(u, p)
            wet = wet_ref[k, rows, :].astype(jnp.float32)
            if side is not None:
                raw_ref[side, 2, k] = u
                rawh_ref[side, 2, k] = unpack(COL_U)
                raw_ref[side, 4, k] = wet
                rawh_ref[side, 4, k] = unpack(COL_WET)
            new = march(
                parts(0, t_ref), parts(1, s_ref), (u, *vertical(u_ref, (k,), r, u)), parts(3, v_ref),
                vertical(p_ref, (), r, p),
                (east_of(to_west, halo, lane), west_of(to_east, halo, lane)),
                wet, coriolis[r],
            )
            for index in range(4):
                y_ref[index, rows, :] = new[index]
            heavy = heaviness(new[0], new[1])
            q_ref[rows, :] = psv[r] + GRAVITY * (run1[r] + 0.5 * heavy)
            run1[r] = run1[r] + heavy
        for r, rows in enumerate(blocks):
            side = side_of.get(r)

            def parts(index):
                own = y_ref[index, rows, :]
                halo = pltpu.roll(z_one[index], shifts[r], 1)
                if side is not None:
                    one_ref[side, index, k] = own
                    oneh_ref[side, index, k] = halo
                return (own, east_of(own, halo, lane), west_of(own, halo, lane), *vertical(y_ref, (index,), r, own))

            p, u = q_ref[rows, :], y_ref[2, rows, :]
            halo = pltpu.roll(z_one_slopes, shifts[r], 1)
            to_west, to_east = slopes(u, p)
            if side is not None:
                one_ref[side, 2, k] = u
                oneh_ref[side, 2, k] = pltpu.roll(z_one[2], shifts[r], 1)
            wet = wet_ref[k, rows, :].astype(jnp.float32)
            new = march(
                parts(0), parts(1), (u, *vertical(y_ref, (2,), r, u)), parts(3),
                vertical(q_ref, (), r, p),
                (east_of(to_west, halo, lane), west_of(to_east, halo, lane)),
                wet, coriolis[r],
            )
            for index in range(4):
                out_ref[index, k, rows, :] = new[index]
            heavy = heaviness(new[0], new[1])
            out_ref[4, k, rows, :] = psv[r] + GRAVITY * (run2[r] + 0.5 * heavy)
            run2[r] = run2[r] + heavy
        return tuple(tuple(x) for x in (run0, run1, run2))

    zero = tuple(jnp.zeros((8, LANES), jnp.float32) for _ in range(BLOCKS))
    running = (zero, zero, zero)
    parts_of = [pl.ds(part * LEVELS // PARTS, LEVELS // PARTS) for part in range(PARTS)]
    for part, levels in enumerate(parts_of):
        running = lax.fori_loop(part * LEVELS // PARTS, (part + 1) * LEVELS // PARTS, level, running)
        for index, out in enumerate(outs):
            pltpu.make_async_copy(out_ref.at[index, levels], out.at[levels], sems.at[part]).start()
    for part, levels in enumerate(parts_of):
        pltpu.make_async_copy(out_ref.at[:, levels], out_ref.at[:, levels], sems.at[part]).wait()


def patch_kernel(
    ps_ref, far_ref, near_ref, raw_ref, rawh_ref, one_ref, oneh_ref, psh_ref, t_in, s_in, u_in, v_in, p_in,
    t_hbm, s_hbm, u_hbm, v_hbm, p_hbm, block_ref, sems,
):
    outs = (t_hbm, s_hbm, u_hbm, v_hbm, p_hbm)
    lat = lax.axis_index("lat")
    even = lat % 2 == 0
    lane = lanes_of((LEVELS, LANES))
    depth = lax.broadcasted_iota(jnp.int32, (LEVELS, LANES), 0)
    near, far = near_ref[...], far_ref[...]
    south = jnp.where(lat == 0, 0.0, jnp.where(even, far, near))
    north = jnp.where(even, near, far)

    def pressure(t, s, ps):
        heavy = heaviness(t, s)
        total = heavy
        for shift in (1, 2, 4, 8):
            total = total + jnp.where(depth >= shift, pltpu.roll(total, shift, 0), 0.0)
        return ps + GRAVITY * (total - 0.5 * heavy)

    def side_rows(side, value):
        rows = (0, 1, 2) if side == 0 else (7, 6, 5)
        at = [side * (ROWS - 8) + r for r in rows]
        block = BLOCKS - 1 if side == 0 else 0

        def unfold(row):
            row = jnp.broadcast_to(pltpu.roll(row, LANES - 2 * (block + 1), 1), (LEVELS, LANES))
            for bit in (1, 2, 4, 8):
                row = jnp.where(depth & bit != 0, pltpu.roll(row, LANES - 8 * bit, 1), row)
            return row

        def five(own, halo, out, inn):
            ns = (inn, out) if side == 0 else (out, inn)
            return (own, east_of(own, halo, lane), west_of(own, halo, lane), *ns)

        def five_halo(own, halo, out, inn):
            ns = (inn, out) if side == 0 else (out, inn)
            return (halo, east_of(halo, own, lane), west_of(halo, own, lane), *ns)

        ring2 = [value[(2 * i + 1) * LEVELS : (2 * i + 2) * LEVELS] for i in range(4)]
        ring1 = [value[2 * i * LEVELS : (2 * i + 1) * LEVELS] for i in range(4)]
        corner = [unfold(value[ROW_CORNER + i : ROW_CORNER + i + 1]) for i in range(5)]
        edge0 = [raw_ref[side, i, :, rows[0], :] for i in range(5)]
        edge0h = [rawh_ref[side, i, :, rows[0], :] for i in range(5)]
        edge1 = [raw_ref[side, i, :, rows[1], :] for i in range(5)]
        edge1h = [rawh_ref[side, i, :, rows[1], :] for i in range(4)]
        one1 = [one_ref[side, i, :, rows[1], :] for i in range(4)]
        one1h = [oneh_ref[side, i, :, rows[1], :] for i in range(4)]
        one2 = [one_ref[side, i, :, rows[2], :] for i in range(4)]
        wet_ring = value[ROW_WET : ROW_WET + LEVELS]
        ps_ring2, ps_ring1 = value[ROW_PS + 1 : ROW_PS + 2], value[ROW_PS : ROW_PS + 1]
        ps_corner = corner[4][0:1]
        ps0, ps1, ps2 = (ps_ref[pl.ds(a, 1), :] for a in at)
        ps0h, ps1h = (psh_ref[side, pl.ds(r, 1), :] for r in rows[:2])
        step = -1 if side == 0 else 1
        cor_ring, cor0, cor1 = (coriolis_of(jnp.int32(at[0] + d)) for d in (step, 0, -step))

        p_ring2 = pressure(ring2[0], ring2[1], ps_ring2)
        p_ring1 = pressure(ring1[0], ring1[1], ps_ring1)
        p_corner = pressure(corner[0], corner[1], ps_corner)
        p0 = pressure(edge0[0], edge0[1], ps0)
        p0h = pressure(edge0h[0], edge0h[1], ps0h)
        p1 = pressure(edge1[0], edge1[1], ps1)
        p1h = pressure(edge1h[0], edge1h[1], ps1h)

        def sides_of(u, uh, p, ph):
            west, east = slopes(u, p)
            west_halo, east_halo = slopes(uh, ph)
            return (
                (east_of(west, west_halo, lane), west_of(east, east_halo, lane)),
                (east_of(west_halo, west, lane), west_of(east_halo, east, lane)),
            )

        def ns(out, inn):
            return (inn, out) if side == 0 else (out, inn)

        sides_ring, _ = sides_of(ring1[2], corner[2], p_ring1, p_corner)
        sides0, sides0h = sides_of(edge0[2], edge0h[2], p0, p0h)
        first_ring = march(
            *(five(ring1[i], corner[i], ring2[i], edge0[i]) for i in range(2)),
            (ring1[2], *ns(ring2[2], edge0[2])),
            five(ring1[3], corner[3], ring2[3], edge0[3]),
            ns(p_ring2, p0), sides_ring, wet_ring, cor_ring,
        )
        first0 = march(
            *(five(edge0[i], edge0h[i], ring1[i], edge1[i]) for i in range(2)),
            (edge0[2], *ns(ring1[2], edge1[2])),
            five(edge0[3], edge0h[3], ring1[3], edge1[3]),
            ns(p_ring1, p1), sides0, edge0[4], cor0,
        )
        first0h = march(
            *(five_halo(edge0[i], edge0h[i], corner[i], edge1h[i]) for i in range(2)),
            (edge0h[2], *ns(corner[2], edge1h[2])),
            five_halo(edge0[3], edge0h[3], corner[3], edge1h[3]),
            ns(p_corner, p1h), sides0h, edge0h[4], cor0,
        )
        p_ring1 = pressure(first_ring[0], first_ring[1], ps_ring1)
        p0 = pressure(first0[0], first0[1], ps0)
        p0h = pressure(first0h[0], first0h[1], ps0h)
        p1 = pressure(one1[0], one1[1], ps1)
        p1h = pressure(one1h[0], one1h[1], ps1h)
        p2 = pressure(one2[0], one2[1], ps2)
        sides0, _ = sides_of(first0[2], first0h[2], p0, p0h)
        sides1, _ = sides_of(one1[2], one1h[2], p1, p1h)
        second0 = march(
            *(five(first0[i], first0h[i], first_ring[i], one1[i]) for i in range(2)),
            (first0[2], *ns(first_ring[2], one1[2])),
            five(first0[3], first0h[3], first_ring[3], one1[3]),
            ns(p_ring1, p1), sides0, edge0[4], cor0,
        )
        second1 = march(
            *(five(one1[i], one1h[i], first0[i], one2[i]) for i in range(2)),
            (one1[2], *ns(first0[2], one2[2])),
            five(one1[3], one1h[3], first0[3], one2[3]),
            ns(p0, p2), sides1, edge1[4], cor1,
        )
        second0 = (*second0, pressure(second0[0], second0[1], ps0))
        second1 = (*second1, pressure(second1[0], second1[1], ps1))
        for index, out in enumerate(outs):
            block_ref[side, index, :, side, :] = second0[index]
            block_ref[side, index, :, 1 - side, :] = second1[index]
            pltpu.make_async_copy(
                block_ref.at[side, index], out.at[:, pl.ds(side * (ROWS - 2), 2), :], sems.at[0]
            ).start()

    side_rows(0, south)
    side_rows(1, north)
    pltpu.make_async_copy(block_ref, block_ref, sems.at[0]).wait()


def exchanges(lon_count, lat_count):
    def at(lat, lon):
        return (lon % lon_count) * lat_count + lat

    def lat_far(lat, lon):
        if lat == 0:
            return at(0, lon ^ 1)
        if lat == lat_count - 1:
            return at(lat, lon_count - 1 - lon)
        return at(lat + 1 if lat % 2 else lat - 1, lon)

    cells = [(lat, lon) for lat in range(lat_count) for lon in range(lon_count)]
    lon_near = [(at(a, o), at(a, o ^ 1)) for a, o in cells]
    lon_far = [(at(a, o), at(a, o + 1 if o % 2 else o - 1)) for a, o in cells]
    lat_near = [(at(a, o), at(a ^ 1, o)) for a, o in cells]
    return lon_near, lon_far, lat_near, [(at(a, o), lat_far(a, o)) for a, o in cells]


def swap(value, pairs):
    return lax.ppermute(value, ("lon", "lat"), pairs)


def on_device(t, s, u, v, ps, wet):
    lon_near, lon_far, lat_near, lat_far = exchanges(lax.axis_size("lon"), lax.axis_size("lat"))
    inputs = (t, s, u, v, ps, wet)
    kept = [pltpu.with_memory_space_constraint(x, pltpu.HBM) for x in inputs]
    cols = jax.ShapeDtypeStruct((COL_ROWS, LANES), jnp.float32)
    rows = jax.ShapeDtypeStruct((ROW_ROWS, LANES), jnp.float32)

    def grant(mib):
        return pltpu.CompilerParams(vmem_limit_bytes=int(mib * 1024 * 1024))

    col_near, col_far = pl.pallas_call(
        pack_columns,
        out_shape=(cols, cols),
        in_specs=[HBM] * 6,
        out_specs=(VMEM, VMEM),
        scratch_shapes=[
            pltpu.VMEM((4, *t.shape), jnp.float32),
            pltpu.VMEM(wet.shape, wet.dtype),
            pltpu.VMEM(ps.shape, jnp.float32),
            pltpu.SemaphoreType.DMA((3,)),
        ],
        compiler_params=grant(6),
    )(*kept)
    block = (LEVELS, 8, LANES)
    row_near, row_far = pl.pallas_call(
        pack_rows,
        out_shape=(rows, rows),
        in_specs=[HBM] * 6,
        out_specs=(VMEM, VMEM),
        scratch_shapes=[
            pltpu.VMEM((2, 4, *block), jnp.float32),
            pltpu.VMEM((2, *block), jnp.int32),
            pltpu.VMEM((ROWS, LANES), jnp.float32),
            pltpu.SemaphoreType.DMA((3,)),
        ],
        compiler_params=grant(4),
    )(*kept)
    got_far = swap(col_far, lon_far)
    got_near = swap(col_near, lon_near)
    row_far, row_near = pl.pallas_call(
        pack_corners,
        out_shape=(rows, rows),
        in_specs=[VMEM] * 4,
        out_specs=(VMEM, VMEM),
        input_output_aliases={2: 0, 3: 1},
        compiler_params=grant(2),
    )(got_far, got_near, row_far, row_near)
    row_far = swap(row_far, lat_far)
    row_near = swap(row_near, lat_near)
    out = jax.ShapeDtypeStruct(t.shape, jnp.float32)

    def blocks(count):
        return jax.ShapeDtypeStruct((2, count, *block), jnp.float32)

    plane = pltpu.VMEM((ROWS, LANES), jnp.float32)
    *outs, raw, raw_halo, one, one_halo, ps_halo = pl.pallas_call(
        main_kernel,
        out_shape=(out,) * 5 + (blocks(5), blocks(5), blocks(4), blocks(4), jax.ShapeDtypeStruct((2, 8, LANES), jnp.float32)),
        in_specs=[VMEM] * 10,
        out_specs=(HBM,) * 5 + (VMEM,) * 5,
        scratch_shapes=[
            plane,
            pltpu.VMEM((4, ROWS, LANES), jnp.float32),
            plane,
            pltpu.VMEM((5, *t.shape), jnp.float32),
            pltpu.SemaphoreType.DMA((PARTS,)),
        ],
        compiler_params=grant(12),
    )(*inputs, got_near, got_far, col_near, col_far)
    return pl.pallas_call(
        patch_kernel,
        out_shape=(out,) * 5,
        in_specs=[VMEM] * 8 + [HBM] * 5,
        out_specs=(HBM,) * 5,
        scratch_shapes=[
            pltpu.VMEM((2, 5, LEVELS, 2, LANES), jnp.float32),
            pltpu.SemaphoreType.DMA((1,)),
        ],
        input_output_aliases={8 + i: i for i in range(5)},
        compiler_params=grant(8),
    )(ps, row_far, row_near, raw, raw_halo, one, one_halo, ps_halo, *outs)


def solution(mesh):
    field = P(None, "lat", "lon")
    return jax.shard_map(
        on_device,
        mesh=mesh,
        in_specs=(field, field, field, field, P("lat", "lon"), field),
        out_specs=(field,) * 5,
        check_vma=False,
    )
```

```python
import jax
import jax.numpy as jnp
from jax import lax
from jax.experimental import pallas as pl
from jax.experimental.pallas import tpu as pltpu
from jax.sharding import PartitionSpec as P

STEPS = 2
HEAT_EXPANSION = 0.2
SALT_CONTRACTION = 0.15
GRAVITY = 0.5
TIME_STEP = 0.2
VISCOSITY = 0.25
DIFFUSIVITY = 0.2
ROTATION = 1.0

LEVELS = 16
ROWS = 32
LANES = 128
BLOCKS = ROWS // 8
SLOTS = LEVELS * BLOCKS

COL_T, COL_S, COL_U, COL_V, COL_WET, COL_PS = range(6)
COL_TILE = 8
COL_ROWS = 6 * COL_TILE
ROW_WET = 4 * 2 * LEVELS
ROW_PS = ROW_WET + LEVELS
ROW_CORNER = ROW_PS + 8
ROW_ROWS = ROW_CORNER + 8

PARTS = ((0, 8), (8, 14), (14, 16))

VMEM = pl.BlockSpec(memory_space=pltpu.VMEM)
HBM = pl.BlockSpec(memory_space=pltpu.HBM)


def lanes_of(shape):
    return lax.broadcasted_iota(jnp.int32, shape, len(shape) - 1)


def pack_columns(
    t_hbm, s_hbm, u_hbm, v_hbm, ps_hbm, wet_hbm, near_ref, far_ref, x_ref, wet_ref, ps_ref, sems
):
    for index, src in enumerate((t_hbm, s_hbm, u_hbm, v_hbm)):
        pltpu.make_async_copy(src, x_ref.at[index], sems.at[0]).start()
    rest = (
        pltpu.make_async_copy(wet_hbm, wet_ref, sems.at[1]),
        pltpu.make_async_copy(ps_hbm, ps_ref, sems.at[2]),
    )
    for copy in rest:
        copy.start()
    even = lax.axis_index("lon") % 2 == 0
    slot = lanes_of((8, LANES)) >> 1
    masks = [slot == j for j in range(SLOTS)]

    def pack(index, tiles):
        east = jnp.zeros((8, LANES), jnp.float32)
        west = jnp.zeros((8, LANES), jnp.float32)
        for j, tile in enumerate(tiles):
            rolled = pltpu.roll(tile(), (2 * j + 2) % LANES, 1)
            east = jnp.where(masks[j], rolled, east)
            west = jnp.where(masks[(j + 1) % SLOTS], rolled, west)
        rows = pl.ds(index * COL_TILE, COL_TILE)
        near_ref[rows, :] = jnp.where(even, east, west)
        far_ref[rows, :] = jnp.where(even, west, east)

    def tiles_of(ref):
        return [
            (lambda j=j: ref[j // BLOCKS, pl.ds(8 * (j % BLOCKS), 8), :].astype(jnp.float32))
            for j in range(SLOTS)
        ]

    pltpu.make_async_copy(x_ref, x_ref, sems.at[0]).wait()
    for index in range(4):
        pack(index, tiles_of(x_ref.at[index]))
    for copy in rest:
        copy.wait()
    pack(COL_WET, tiles_of(wet_ref))
    pack(COL_PS, [(lambda r=r: ps_ref[pl.ds(8 * r, 8), :]) for r in range(BLOCKS)])


def reverse_lanes(value):
    index = LANES - 1 - lanes_of(value.shape)
    return jnp.take_along_axis(value, index, axis=1, mode="promise_in_bounds")


def pack_rows(
    t_hbm, s_hbm, u_hbm, v_hbm, ps_hbm, wet_hbm, near_ref, far_ref, x_ref, wet_ref, ps_ref, sems
):
    rest = pltpu.make_async_copy(ps_hbm, ps_ref, sems.at[2])
    rest.start()
    for side, first in ((0, 0), (1, ROWS - 8)):
        for index, src in enumerate((t_hbm, s_hbm, u_hbm, v_hbm)):
            pltpu.make_async_copy(src.at[:, pl.ds(first, 8), :], x_ref.at[side, index], sems.at[0]).start()
        pltpu.make_async_copy(wet_hbm.at[:, pl.ds(first, 8), :], wet_ref.at[side], sems.at[1]).start()
    lat = lax.axis_index("lat")
    even = lat % 2 == 0
    fold = lat == lax.axis_size("lat") - 1
    for ref, sem in ((x_ref, 0), (wet_ref, 1)):
        pltpu.make_async_copy(ref, ref, sems.at[sem]).wait()
    rest.wait()

    def put(first, north, south, sign):
        rows = pl.ds(first, north.shape[0])
        near_ref[rows, :] = jnp.where(even, north, south)
        far_ref[rows, :] = jnp.where(even, south, north)

        @pl.when(fold)
        def _():
            far_ref[rows, :] = sign * reverse_lanes(north)

    for index, sign in enumerate((1.0, 1.0, -1.0, -1.0)):
        for ring in range(2):
            put((2 * index + ring) * LEVELS, x_ref[1, index, :, 7 - ring, :], x_ref[0, index, :, ring, :], sign)
    put(ROW_WET, wet_ref[1, :, 7, :].astype(jnp.float32), wet_ref[0, :, 0, :].astype(jnp.float32), 1.0)
    top, bottom = ps_ref[pl.ds(ROWS - 8, 8), :], ps_ref[pl.ds(0, 8), :]
    sub = lax.broadcasted_iota(jnp.int32, (8, LANES), 0)
    north = jnp.where(sub == 0, pltpu.roll(top, 1, 0), pltpu.roll(top, 3, 0))
    put(ROW_PS, north, bottom, 1.0)
    near_ref[pl.ds(ROW_CORNER, 8), :] = jnp.zeros((8, LANES), jnp.float32)
    far_ref[pl.ds(ROW_CORNER, 8), :] = jnp.zeros((8, LANES), jnp.float32)


def halo_tiles(near, far, even_lon):
    slot = lanes_of(near.shape) >> 1
    west = jnp.where(even_lon, far, near)
    east = jnp.where(even_lon, near, far)
    return (
        jnp.where(slot % 2 == 0, west, east),
        jnp.where(slot % 2 == 0, east, west),
    )


def pack_corners(far_ref, near_ref, far_in, near_in, far_out, near_out):
    lat = lax.axis_index("lat")
    even = lat % 2 == 0
    fold = lat == lax.axis_size("lat") - 1
    even_tile, odd_tile = halo_tiles(near_ref[...], far_ref[...], lax.axis_index("lon") % 2 == 0)
    lane = lanes_of((8, LANES))
    sub = lax.broadcasted_iota(jnp.int32, (8, LANES), 0)

    def gather(tile, row):
        out = jnp.zeros((8, LANES), jnp.float32)
        for index, field in enumerate((COL_T, COL_S, COL_U, COL_V, COL_PS)):
            one = pltpu.roll(tile[field * COL_TILE : (field + 1) * COL_TILE], (index - row) % 8, 0)
            out = jnp.where(sub == index, one, out)
        return out

    north, south = gather(odd_tile, 7), gather(even_tile, 0)
    mirrored = pltpu.roll(north, LANES - 6, 1)
    mirrored = jnp.where(lane % 2 == 0, pltpu.roll(mirrored, 1, 1), pltpu.roll(mirrored, LANES - 1, 1))
    mirrored = jnp.where((sub == 2) | (sub == 3), -mirrored, mirrored)
    rows = pl.ds(ROW_CORNER, 8)
    near_out[rows, :] = jnp.where(even, north, south)
    far_out[rows, :] = jnp.where(fold, mirrored, jnp.where(even, south, north))


def laplace(q):
    centre, east, west, north, south = q
    return east + west + north + south - 4.0 * centre


def slopes(u, p):
    return VISCOSITY * u - 0.5 * p, VISCOSITY * u + 0.5 * p


def march(t, s, u, v, p, sides, wet, coriolis):
    grad_y = 0.5 * (p[0] - p[1])

    def tracer(q):
        transport = -0.5 * (u[0] * (q[1] - q[2]) + v[0] * (q[3] - q[4]))
        return wet * (q[0] + TIME_STEP * (transport + DIFFUSIVITY * laplace(q)))

    push = sides[0] + sides[1] + VISCOSITY * (u[1] + u[2]) - 4.0 * VISCOSITY * u[0]
    return (
        tracer(t),
        tracer(s),
        wet * (u[0] + TIME_STEP * (coriolis * v[0] + push)),
        wet * (v[0] + TIME_STEP * (-coriolis * u[0] - grad_y + VISCOSITY * laplace(v))),
    )


def heaviness(t, s):
    return -HEAT_EXPANSION * t + SALT_CONTRACTION * s


def coriolis_of(row):
    total = ROWS * lax.axis_size("lat")
    row = jnp.minimum(lax.axis_index("lat") * ROWS + row, total - 1).astype(jnp.float32)
    return ROTATION * (2.0 * (row + 0.5) / total - 1.0)


def east_of(own, halo, lane):
    return pltpu.roll(jnp.where(lane == 0, halo, own), LANES - 1, 1)


def west_of(own, halo, lane):
    return pltpu.roll(jnp.where(lane == LANES - 1, halo, own), 1, 1)


def packed_pressure(t, s, ps, order):
    heavy = heaviness(t, s)
    total = heavy
    for shift in (8, 16, 32, 64):
        total = total + jnp.where(order >= shift, pltpu.roll(total, shift, 1), 0.0)
        ps = ps + pltpu.roll(ps, shift, 1)
    return ps + GRAVITY * (total - 0.5 * heavy)


def main_kernel(
    t_ref, s_ref, u_ref, v_ref, ps_ref, wet_ref, near_ref, far_ref, own_near_ref, own_far_ref,
    t_hbm, s_hbm, u_hbm, v_hbm, p_hbm, raw_ref, rawh_ref, one_ref, oneh_ref, psh_ref,
    p_ref, y_ref, q_ref, out_ref, sems,
):
    even = lax.axis_index("lon") % 2 == 0
    near, far = near_ref[...], far_ref[...]
    own_near, own_far = own_near_ref[...], own_far_ref[...]
    own_east, own_west = jnp.where(even, own_near, own_far), jnp.where(even, own_far, own_near)
    got_west, got_east = jnp.where(even, far, near), jnp.where(even, near, far)
    odd = lanes_of(near.shape) % 2 == 1
    even_tile, odd_tile = halo_tiles(near, far, even)

    z = jnp.where(odd, got_west, got_east)
    z_east = pltpu.roll(jnp.where(odd, got_east, own_west), LANES - 1, 1)
    z_west = pltpu.roll(jnp.where(odd, own_east, got_west), 1, 1)
    lane = lanes_of((8, LANES))
    sub = lax.broadcasted_iota(jnp.int32, (8, LANES), 0)
    order = (lane + LANES - 1) % LANES

    def tile(value, index):
        return value[index * COL_TILE : (index + 1) * COL_TILE]

    def above(q):
        return jnp.where(sub == 7, pltpu.roll(pltpu.roll(q, LANES - 2, 1), 7, 0), pltpu.roll(q, 7, 0))

    def below(q):
        return jnp.where(sub == 0, pltpu.roll(pltpu.roll(q, 2, 1), 1, 0), pltpu.roll(q, 1, 0))

    zp, zp_east, zp_west = (
        packed_pressure(tile(q, COL_T), tile(q, COL_S), tile(q, COL_PS), order) for q in (z, z_east, z_west)
    )

    def centred(q):
        return q, above(q), below(q)

    def around(index):
        q = tile(z, index)
        return q, tile(z_east, index), tile(z_west, index), above(q), below(q)

    z_one = march(
        around(COL_T), around(COL_S), centred(tile(z, COL_U)), around(COL_V),
        (above(zp), below(zp)),
        (slopes(tile(z_east, COL_U), zp_east)[0], slopes(tile(z_west, COL_U), zp_west)[1]),
        tile(z, COL_WET),
        coriolis_of(8 * ((order // 2) % BLOCKS) + sub),
    )
    zp_one = packed_pressure(z_one[0], z_one[1], tile(z, COL_PS), order)

    def packed_slopes(u, p):
        to_west, to_east = slopes(u, p)
        return jnp.where(lane % 2 == 1, to_east, to_west)

    z_slopes = packed_slopes(tile(z, COL_U), zp)
    z_one_slopes = packed_slopes(z_one[2], zp_one)

    for side, block, tiles in ((0, 0, even_tile), (1, BLOCKS - 1, odd_tile)):
        psh_ref[side] = pltpu.roll(tile(tiles, COL_PS), LANES - 2 * (block + 1), 1)

    outs = (t_hbm, s_hbm, u_hbm, v_hbm, p_hbm)
    blocks = [pl.ds(8 * r, 8) for r in range(BLOCKS)]
    coriolis = [coriolis_of(8 * r + sub) for r in range(BLOCKS)]
    psv = [ps_ref[rows, :] for rows in blocks]

    def vertical(ref, lead, r, centre):
        north = ref[(*lead, pl.ds(8 * r + 1, 8))] if r < BLOCKS - 1 else pltpu.roll(centre, 7, 0)
        south = ref[(*lead, pl.ds(8 * r - 1, 8))] if r > 0 else pltpu.roll(centre, 1, 0)
        return north, south

    def level(k, running, half=0):
        run0, run1, run2 = (list(x) for x in running)
        side_of = {0: 0, BLOCKS - 1: 1}
        shifts = [LANES - 2 - 8 * k - 2 * r for r in range(BLOCKS)]
        for r, rows in enumerate(blocks):
            heavy = heaviness(t_ref[k, rows, :], s_ref[k, rows, :])
            p_ref[half, rows, :] = psv[r] + GRAVITY * (run0[r] + 0.5 * heavy)
            run0[r] = run0[r] + heavy
        for r, rows in enumerate(blocks):
            tiles = odd_tile if r % 2 else even_tile
            side = side_of.get(r)

            def unpack(index):
                return pltpu.roll(tile(tiles, index), shifts[r], 1)

            def parts(index, ref):
                own, halo = ref[k, rows, :], unpack(index)
                if side is not None:
                    raw_ref[side, index, k] = own
                    rawh_ref[side, index, k] = halo
                return (own, east_of(own, halo, lane), west_of(own, halo, lane), *vertical(ref, (k,), r, own))

            p, u = p_ref[half, rows, :], u_ref[k, rows, :]
            halo = pltpu.roll(z_slopes, shifts[r], 1)
            to_west, to_east = slopes(u, p)
            wet = wet_ref[k, rows, :].astype(jnp.float32)
            if side is not None:
                raw_ref[side, 2, k] = u
                rawh_ref[side, 2, k] = unpack(COL_U)
                raw_ref[side, 4, k] = wet
                rawh_ref[side, 4, k] = unpack(COL_WET)
            new = march(
                parts(0, t_ref), parts(1, s_ref), (u, *vertical(u_ref, (k,), r, u)), parts(3, v_ref),
                vertical(p_ref, (half,), r, p),
                (east_of(to_west, halo, lane), west_of(to_east, halo, lane)),
                wet, coriolis[r],
            )
            for index in range(4):
                y_ref[half, index, rows, :] = new[index]
            heavy = heaviness(new[0], new[1])
            q_ref[half, rows, :] = psv[r] + GRAVITY * (run1[r] + 0.5 * heavy)
            run1[r] = run1[r] + heavy
        for r, rows in enumerate(blocks):
            side = side_of.get(r)

            def parts(index):
                own = y_ref[half, index, rows, :]
                halo = pltpu.roll(z_one[index], shifts[r], 1)
                if side is not None:
                    one_ref[side, index, k] = own
                    oneh_ref[side, index, k] = halo
                return (own, east_of(own, halo, lane), west_of(own, halo, lane), *vertical(y_ref, (half, index), r, own))

            p, u = q_ref[half, rows, :], y_ref[half, 2, rows, :]
            halo = pltpu.roll(z_one_slopes, shifts[r], 1)
            to_west, to_east = slopes(u, p)
            if side is not None:
                one_ref[side, 2, k] = u
                oneh_ref[side, 2, k] = pltpu.roll(z_one[2], shifts[r], 1)
            wet = wet_ref[k, rows, :].astype(jnp.float32)
            new = march(
                parts(0), parts(1), (u, *vertical(y_ref, (half, 2), r, u)), parts(3),
                vertical(q_ref, (half,), r, p),
                (east_of(to_west, halo, lane), west_of(to_east, halo, lane)),
                wet, coriolis[r],
            )
            for index in range(4):
                out_ref[index, k, rows, :] = new[index]
            heavy = heaviness(new[0], new[1])
            out_ref[4, k, rows, :] = psv[r] + GRAVITY * (run2[r] + 0.5 * heavy)
            run2[r] = run2[r] + heavy
        return tuple(tuple(x) for x in (run0, run1, run2))

    zero = tuple(jnp.zeros((8, LANES), jnp.float32) for _ in range(BLOCKS))
    running = (zero, zero, zero)
    def pair(k, running):
        return level(2 * k + 1, level(2 * k, running, 0), 1)

    for part, (first, last) in enumerate(PARTS):
        running = lax.fori_loop(first // 2, last // 2, pair, running)
        for index, out in enumerate(outs):
            levels = pl.ds(first, last - first)
            pltpu.make_async_copy(out_ref.at[index, levels], out.at[levels], sems.at[part]).start()
    for part, (first, last) in enumerate(PARTS):
        whole = out_ref.at[:, pl.ds(first, last - first)]
        pltpu.make_async_copy(whole, whole, sems.at[part]).wait()


def patch_kernel(
    ps_ref, far_ref, near_ref, raw_ref, rawh_ref, one_ref, oneh_ref, psh_ref, t_in, s_in, u_in, v_in, p_in,
    t_hbm, s_hbm, u_hbm, v_hbm, p_hbm, block_ref, sems,
):
    outs = (t_hbm, s_hbm, u_hbm, v_hbm, p_hbm)
    lat = lax.axis_index("lat")
    even = lat % 2 == 0
    lane = lanes_of((LEVELS, LANES))
    depth = lax.broadcasted_iota(jnp.int32, (LEVELS, LANES), 0)
    near, far = near_ref[...], far_ref[...]
    south = jnp.where(lat == 0, 0.0, jnp.where(even, far, near))
    north = jnp.where(even, near, far)

    def pressure(t, s, ps):
        heavy = heaviness(t, s)
        total = heavy
        for shift in (1, 2, 4, 8):
            total = total + jnp.where(depth >= shift, pltpu.roll(total, shift, 0), 0.0)
        return ps + GRAVITY * (total - 0.5 * heavy)

    def side_rows(side, value):
        rows = (0, 1, 2) if side == 0 else (7, 6, 5)
        at = [side * (ROWS - 8) + r for r in rows]
        block = BLOCKS - 1 if side == 0 else 0

        def unfold(row):
            row = jnp.broadcast_to(pltpu.roll(row, LANES - 2 * (block + 1), 1), (LEVELS, LANES))
            for bit in (1, 2, 4, 8):
                row = jnp.where(depth & bit != 0, pltpu.roll(row, LANES - 8 * bit, 1), row)
            return row

        def five(own, halo, out, inn):
            ns = (inn, out) if side == 0 else (out, inn)
            return (own, east_of(own, halo, lane), west_of(own, halo, lane), *ns)

        def five_halo(own, halo, out, inn):
            ns = (inn, out) if side == 0 else (out, inn)
            return (halo, east_of(halo, own, lane), west_of(halo, own, lane), *ns)

        ring2 = [value[(2 * i + 1) * LEVELS : (2 * i + 2) * LEVELS] for i in range(4)]
        ring1 = [value[2 * i * LEVELS : (2 * i + 1) * LEVELS] for i in range(4)]
        corner = [unfold(value[ROW_CORNER + i : ROW_CORNER + i + 1]) for i in range(5)]
        edge0 = [raw_ref[side, i, :, rows[0], :] for i in range(5)]
        edge0h = [rawh_ref[side, i, :, rows[0], :] for i in range(5)]
        edge1 = [raw_ref[side, i, :, rows[1], :] for i in range(5)]
        edge1h = [rawh_ref[side, i, :, rows[1], :] for i in range(4)]
        one1 = [one_ref[side, i, :, rows[1], :] for i in range(4)]
        one1h = [oneh_ref[side, i, :, rows[1], :] for i in range(4)]
        one2 = [one_ref[side, i, :, rows[2], :] for i in range(4)]
        wet_ring = value[ROW_WET : ROW_WET + LEVELS]
        ps_ring2, ps_ring1 = value[ROW_PS + 1 : ROW_PS + 2], value[ROW_PS : ROW_PS + 1]
        ps_corner = corner[4][0:1]
        ps0, ps1, ps2 = (ps_ref[pl.ds(a, 1), :] for a in at)
        ps0h, ps1h = (psh_ref[side, pl.ds(r, 1), :] for r in rows[:2])
        step = -1 if side == 0 else 1
        cor_ring, cor0, cor1 = (coriolis_of(jnp.int32(at[0] + d)) for d in (step, 0, -step))

        p_ring2 = pressure(ring2[0], ring2[1], ps_ring2)
        p_ring1 = pressure(ring1[0], ring1[1], ps_ring1)
        p_corner = pressure(corner[0], corner[1], ps_corner)
        p0 = pressure(edge0[0], edge0[1], ps0)
        p0h = pressure(edge0h[0], edge0h[1], ps0h)
        p1 = pressure(edge1[0], edge1[1], ps1)
        p1h = pressure(edge1h[0], edge1h[1], ps1h)

        def sides_of(u, uh, p, ph):
            west, east = slopes(u, p)
            west_halo, east_halo = slopes(uh, ph)
            return (
                (east_of(west, west_halo, lane), west_of(east, east_halo, lane)),
                (east_of(west_halo, west, lane), west_of(east_halo, east, lane)),
            )

        def ns(out, inn):
            return (inn, out) if side == 0 else (out, inn)

        sides_ring, _ = sides_of(ring1[2], corner[2], p_ring1, p_corner)
        sides0, sides0h = sides_of(edge0[2], edge0h[2], p0, p0h)
        first_ring = march(
            *(five(ring1[i], corner[i], ring2[i], edge0[i]) for i in range(2)),
            (ring1[2], *ns(ring2[2], edge0[2])),
            five(ring1[3], corner[3], ring2[3], edge0[3]),
            ns(p_ring2, p0), sides_ring, wet_ring, cor_ring,
        )
        first0 = march(
            *(five(edge0[i], edge0h[i], ring1[i], edge1[i]) for i in range(2)),
            (edge0[2], *ns(ring1[2], edge1[2])),
            five(edge0[3], edge0h[3], ring1[3], edge1[3]),
            ns(p_ring1, p1), sides0, edge0[4], cor0,
        )
        first0h = march(
            *(five_halo(edge0[i], edge0h[i], corner[i], edge1h[i]) for i in range(2)),
            (edge0h[2], *ns(corner[2], edge1h[2])),
            five_halo(edge0[3], edge0h[3], corner[3], edge1h[3]),
            ns(p_corner, p1h), sides0h, edge0h[4], cor0,
        )
        p_ring1 = pressure(first_ring[0], first_ring[1], ps_ring1)
        p0 = pressure(first0[0], first0[1], ps0)
        p0h = pressure(first0h[0], first0h[1], ps0h)
        p1 = pressure(one1[0], one1[1], ps1)
        p1h = pressure(one1h[0], one1h[1], ps1h)
        p2 = pressure(one2[0], one2[1], ps2)
        sides0, _ = sides_of(first0[2], first0h[2], p0, p0h)
        sides1, _ = sides_of(one1[2], one1h[2], p1, p1h)
        second0 = march(
            *(five(first0[i], first0h[i], first_ring[i], one1[i]) for i in range(2)),
            (first0[2], *ns(first_ring[2], one1[2])),
            five(first0[3], first0h[3], first_ring[3], one1[3]),
            ns(p_ring1, p1), sides0, edge0[4], cor0,
        )
        second1 = march(
            *(five(one1[i], one1h[i], first0[i], one2[i]) for i in range(2)),
            (one1[2], *ns(first0[2], one2[2])),
            five(one1[3], one1h[3], first0[3], one2[3]),
            ns(p0, p2), sides1, edge1[4], cor1,
        )
        second0 = (*second0, pressure(second0[0], second0[1], ps0))
        second1 = (*second1, pressure(second1[0], second1[1], ps1))
        for index, out in enumerate(outs):
            block_ref[side, index, :, side, :] = second0[index]
            block_ref[side, index, :, 1 - side, :] = second1[index]
            pltpu.make_async_copy(
                block_ref.at[side, index], out.at[:, pl.ds(side * (ROWS - 2), 2), :], sems.at[0]
            ).start()

    side_rows(0, south)
    side_rows(1, north)
    pltpu.make_async_copy(block_ref, block_ref, sems.at[0]).wait()


def exchanges(lon_count, lat_count):
    def at(lat, lon):
        return (lon % lon_count) * lat_count + lat

    def lat_far(lat, lon):
        if lat == 0:
            return at(0, lon ^ 1)
        if lat == lat_count - 1:
            return at(lat, lon_count - 1 - lon)
        return at(lat + 1 if lat % 2 else lat - 1, lon)

    cells = [(lat, lon) for lat in range(lat_count) for lon in range(lon_count)]
    lon_near = [(at(a, o), at(a, o ^ 1)) for a, o in cells]
    lon_far = [(at(a, o), at(a, o + 1 if o % 2 else o - 1)) for a, o in cells]
    lat_near = [(at(a, o), at(a ^ 1, o)) for a, o in cells]
    return lon_near, lon_far, lat_near, [(at(a, o), lat_far(a, o)) for a, o in cells]


def swap(value, pairs):
    return lax.ppermute(value, ("lon", "lat"), pairs)


def on_device(t, s, u, v, ps, wet):
    lon_near, lon_far, lat_near, lat_far = exchanges(lax.axis_size("lon"), lax.axis_size("lat"))
    inputs = (t, s, u, v, ps, wet)
    kept = [pltpu.with_memory_space_constraint(x, pltpu.HBM) for x in inputs]
    cols = jax.ShapeDtypeStruct((COL_ROWS, LANES), jnp.float32)
    rows = jax.ShapeDtypeStruct((ROW_ROWS, LANES), jnp.float32)

    def grant(mib):
        return pltpu.CompilerParams(vmem_limit_bytes=int(mib * 1024 * 1024))

    col_near, col_far = pl.pallas_call(
        pack_columns,
        out_shape=(cols, cols),
        in_specs=[HBM] * 6,
        out_specs=(VMEM, VMEM),
        scratch_shapes=[
            pltpu.VMEM((4, *t.shape), jnp.float32),
            pltpu.VMEM(wet.shape, wet.dtype),
            pltpu.VMEM(ps.shape, jnp.float32),
            pltpu.SemaphoreType.DMA((3,)),
        ],
        compiler_params=grant(6),
    )(*kept)
    block = (LEVELS, 8, LANES)
    row_near, row_far = pl.pallas_call(
        pack_rows,
        out_shape=(rows, rows),
        in_specs=[HBM] * 6,
        out_specs=(VMEM, VMEM),
        scratch_shapes=[
            pltpu.VMEM((2, 4, *block), jnp.float32),
            pltpu.VMEM((2, *block), jnp.int32),
            pltpu.VMEM((ROWS, LANES), jnp.float32),
            pltpu.SemaphoreType.DMA((3,)),
        ],
        compiler_params=grant(4),
    )(*kept)
    got_far = swap(col_far, lon_far)
    got_near = swap(col_near, lon_near)
    row_far, row_near = pl.pallas_call(
        pack_corners,
        out_shape=(rows, rows),
        in_specs=[VMEM] * 4,
        out_specs=(VMEM, VMEM),
        input_output_aliases={2: 0, 3: 1},
        compiler_params=grant(2),
    )(got_far, got_near, row_far, row_near)
    row_far = swap(row_far, lat_far)
    row_near = swap(row_near, lat_near)
    out = jax.ShapeDtypeStruct(t.shape, jnp.float32)

    def blocks(count):
        return jax.ShapeDtypeStruct((2, count, *block), jnp.float32)

    plane = pltpu.VMEM((2, ROWS, LANES), jnp.float32)
    *outs, raw, raw_halo, one, one_halo, ps_halo = pl.pallas_call(
        main_kernel,
        out_shape=(out,) * 5 + (blocks(5), blocks(5), blocks(4), blocks(4), jax.ShapeDtypeStruct((2, 8, LANES), jnp.float32)),
        in_specs=[VMEM] * 10,
        out_specs=(HBM,) * 5 + (VMEM,) * 5,
        scratch_shapes=[
            plane,
            pltpu.VMEM((2, 4, ROWS, LANES), jnp.float32),
            plane,
            pltpu.VMEM((5, *t.shape), jnp.float32),
            pltpu.SemaphoreType.DMA((len(PARTS),)),
        ],
        compiler_params=grant(12),
    )(*inputs, got_near, got_far, col_near, col_far)
    return pl.pallas_call(
        patch_kernel,
        out_shape=(out,) * 5,
        in_specs=[VMEM] * 8 + [HBM] * 5,
        out_specs=(HBM,) * 5,
        scratch_shapes=[
            pltpu.VMEM((2, 5, LEVELS, 2, LANES), jnp.float32),
            pltpu.SemaphoreType.DMA((1,)),
        ],
        input_output_aliases={8 + i: i for i in range(5)},
        compiler_params=grant(8),
    )(ps, row_far, row_near, raw, raw_halo, one, one_halo, ps_halo, *outs)


def solution(mesh):
    field = P(None, "lat", "lon")
    return jax.shard_map(
        on_device,
        mesh=mesh,
        in_specs=(field, field, field, field, P("lat", "lon"), field),
        out_specs=(field,) * 5,
        check_vma=False,
    )
```

```python
import jax
import jax.numpy as jnp
from jax import lax
from jax.experimental import pallas as pl
from jax.experimental.pallas import tpu as pltpu
from jax.sharding import PartitionSpec as P

STEPS = 2
HEAT_EXPANSION = 0.2
SALT_CONTRACTION = 0.15
GRAVITY = 0.5
TIME_STEP = 0.2
VISCOSITY = 0.25
DIFFUSIVITY = 0.2
ROTATION = 1.0

LEVELS = 16
ROWS = 32
LANES = 128
BLOCKS = ROWS // 8
SLOTS = LEVELS * BLOCKS

COL_T, COL_S, COL_U, COL_V, COL_WET, COL_PS = range(6)
COL_TILE = 8
COL_ROWS = 6 * COL_TILE
ROW_WET = 4 * 2 * LEVELS
ROW_PS = ROW_WET + LEVELS
ROW_CORNER = ROW_PS + 8
ROW_ROWS = ROW_CORNER + 8

PARTS = ((0, 8),)
LATE = 8

VMEM = pl.BlockSpec(memory_space=pltpu.VMEM)
HBM = pl.BlockSpec(memory_space=pltpu.HBM)


def lanes_of(shape):
    return lax.broadcasted_iota(jnp.int32, shape, len(shape) - 1)


def pack_columns(
    t_hbm, s_hbm, u_hbm, v_hbm, ps_hbm, wet_hbm, near_ref, far_ref, x_ref, wet_ref, ps_ref, sems
):
    for index, src in enumerate((t_hbm, s_hbm, u_hbm, v_hbm)):
        pltpu.make_async_copy(src, x_ref.at[index], sems.at[0]).start()
    rest = (
        pltpu.make_async_copy(wet_hbm, wet_ref, sems.at[1]),
        pltpu.make_async_copy(ps_hbm, ps_ref, sems.at[2]),
    )
    for copy in rest:
        copy.start()
    even = lax.axis_index("lon") % 2 == 0
    slot = lanes_of((8, LANES)) >> 1
    masks = [slot == j for j in range(SLOTS)]

    def pack(index, tiles):
        east = jnp.zeros((8, LANES), jnp.float32)
        west = jnp.zeros((8, LANES), jnp.float32)
        for j, tile in enumerate(tiles):
            rolled = pltpu.roll(tile(), (2 * j + 2) % LANES, 1)
            east = jnp.where(masks[j], rolled, east)
            west = jnp.where(masks[(j + 1) % SLOTS], rolled, west)
        rows = pl.ds(index * COL_TILE, COL_TILE)
        near_ref[rows, :] = jnp.where(even, east, west)
        far_ref[rows, :] = jnp.where(even, west, east)

    def tiles_of(ref):
        return [
            (lambda j=j: ref[j // BLOCKS, pl.ds(8 * (j % BLOCKS), 8), :].astype(jnp.float32))
            for j in range(SLOTS)
        ]

    pltpu.make_async_copy(x_ref, x_ref, sems.at[0]).wait()
    for index in range(4):
        pack(index, tiles_of(x_ref.at[index]))
    for copy in rest:
        copy.wait()
    pack(COL_WET, tiles_of(wet_ref))
    pack(COL_PS, [(lambda r=r: ps_ref[pl.ds(8 * r, 8), :]) for r in range(BLOCKS)])


def reverse_lanes(value):
    index = LANES - 1 - lanes_of(value.shape)
    return jnp.take_along_axis(value, index, axis=1, mode="promise_in_bounds")


def pack_rows(
    t_hbm, s_hbm, u_hbm, v_hbm, ps_hbm, wet_hbm, near_ref, far_ref, x_ref, wet_ref, ps_ref, sems
):
    rest = pltpu.make_async_copy(ps_hbm, ps_ref, sems.at[2])
    rest.start()
    for side, first in ((0, 0), (1, ROWS - 8)):
        for index, src in enumerate((t_hbm, s_hbm, u_hbm, v_hbm)):
            pltpu.make_async_copy(src.at[:, pl.ds(first, 8), :], x_ref.at[side, index], sems.at[0]).start()
        pltpu.make_async_copy(wet_hbm.at[:, pl.ds(first, 8), :], wet_ref.at[side], sems.at[1]).start()
    lat = lax.axis_index("lat")
    even = lat % 2 == 0
    fold = lat == lax.axis_size("lat") - 1
    for ref, sem in ((x_ref, 0), (wet_ref, 1)):
        pltpu.make_async_copy(ref, ref, sems.at[sem]).wait()
    rest.wait()

    def put(first, north, south, sign):
        rows = pl.ds(first, north.shape[0])
        near_ref[rows, :] = jnp.where(even, north, south)
        far_ref[rows, :] = jnp.where(even, south, north)

        @pl.when(fold)
        def _():
            far_ref[rows, :] = sign * reverse_lanes(north)

    for index, sign in enumerate((1.0, 1.0, -1.0, -1.0)):
        for ring in range(2):
            put((2 * index + ring) * LEVELS, x_ref[1, index, :, 7 - ring, :], x_ref[0, index, :, ring, :], sign)
    put(ROW_WET, wet_ref[1, :, 7, :].astype(jnp.float32), wet_ref[0, :, 0, :].astype(jnp.float32), 1.0)
    top, bottom = ps_ref[pl.ds(ROWS - 8, 8), :], ps_ref[pl.ds(0, 8), :]
    sub = lax.broadcasted_iota(jnp.int32, (8, LANES), 0)
    north = jnp.where(sub == 0, pltpu.roll(top, 1, 0), pltpu.roll(top, 3, 0))
    put(ROW_PS, north, bottom, 1.0)
    near_ref[pl.ds(ROW_CORNER, 8), :] = jnp.zeros((8, LANES), jnp.float32)
    far_ref[pl.ds(ROW_CORNER, 8), :] = jnp.zeros((8, LANES), jnp.float32)


def halo_tiles(near, far, even_lon):
    slot = lanes_of(near.shape) >> 1
    west = jnp.where(even_lon, far, near)
    east = jnp.where(even_lon, near, far)
    return (
        jnp.where(slot % 2 == 0, west, east),
        jnp.where(slot % 2 == 0, east, west),
    )


def pack_corners(far_ref, near_ref, far_in, near_in, far_out, near_out):
    lat = lax.axis_index("lat")
    even = lat % 2 == 0
    fold = lat == lax.axis_size("lat") - 1
    even_tile, odd_tile = halo_tiles(near_ref[...], far_ref[...], lax.axis_index("lon") % 2 == 0)
    lane = lanes_of((8, LANES))
    sub = lax.broadcasted_iota(jnp.int32, (8, LANES), 0)

    def gather(tile, row):
        out = jnp.zeros((8, LANES), jnp.float32)
        for index, field in enumerate((COL_T, COL_S, COL_U, COL_V, COL_PS)):
            one = pltpu.roll(tile[field * COL_TILE : (field + 1) * COL_TILE], (index - row) % 8, 0)
            out = jnp.where(sub == index, one, out)
        return out

    north, south = gather(odd_tile, 7), gather(even_tile, 0)
    mirrored = pltpu.roll(north, LANES - 6, 1)
    mirrored = jnp.where(lane % 2 == 0, pltpu.roll(mirrored, 1, 1), pltpu.roll(mirrored, LANES - 1, 1))
    mirrored = jnp.where((sub == 2) | (sub == 3), -mirrored, mirrored)
    rows = pl.ds(ROW_CORNER, 8)
    near_out[rows, :] = jnp.where(even, north, south)
    far_out[rows, :] = jnp.where(fold, mirrored, jnp.where(even, south, north))


def laplace(q):
    centre, east, west, north, south = q
    return east + west + north + south - 4.0 * centre


def slopes(u, p):
    return VISCOSITY * u - 0.5 * p, VISCOSITY * u + 0.5 * p


def march(t, s, u, v, p, sides, wet, coriolis):
    grad_y = 0.5 * (p[0] - p[1])

    def tracer(q):
        transport = -0.5 * (u[0] * (q[1] - q[2]) + v[0] * (q[3] - q[4]))
        return wet * (q[0] + TIME_STEP * (transport + DIFFUSIVITY * laplace(q)))

    push = sides[0] + sides[1] + VISCOSITY * (u[1] + u[2]) - 4.0 * VISCOSITY * u[0]
    return (
        tracer(t),
        tracer(s),
        wet * (u[0] + TIME_STEP * (coriolis * v[0] + push)),
        wet * (v[0] + TIME_STEP * (-coriolis * u[0] - grad_y + VISCOSITY * laplace(v))),
    )


def heaviness(t, s):
    return -HEAT_EXPANSION * t + SALT_CONTRACTION * s


def coriolis_of(row):
    total = ROWS * lax.axis_size("lat")
    row = jnp.minimum(lax.axis_index("lat") * ROWS + row, total - 1).astype(jnp.float32)
    return ROTATION * (2.0 * (row + 0.5) / total - 1.0)


def east_of(own, halo, lane):
    return pltpu.roll(jnp.where(lane == 0, halo, own), LANES - 1, 1)


def west_of(own, halo, lane):
    return pltpu.roll(jnp.where(lane == LANES - 1, halo, own), 1, 1)


def packed_pressure(t, s, ps, order):
    heavy = heaviness(t, s)
    total = heavy
    for shift in (8, 16, 32, 64):
        total = total + jnp.where(order >= shift, pltpu.roll(total, shift, 1), 0.0)
        ps = ps + pltpu.roll(ps, shift, 1)
    return ps + GRAVITY * (total - 0.5 * heavy)


def main_kernel(
    t_ref, s_ref, u_ref, v_ref, ps_ref, wet_ref, near_ref, far_ref, own_near_ref, own_far_ref,
    t_hbm, s_hbm, u_hbm, v_hbm, p_hbm, raw_ref, rawh_ref, one_ref, oneh_ref, psh_ref, late_ref,
    p_ref, y_ref, q_ref, out_ref, sems,
):
    even = lax.axis_index("lon") % 2 == 0
    near, far = near_ref[...], far_ref[...]
    own_near, own_far = own_near_ref[...], own_far_ref[...]
    own_east, own_west = jnp.where(even, own_near, own_far), jnp.where(even, own_far, own_near)
    got_west, got_east = jnp.where(even, far, near), jnp.where(even, near, far)
    odd = lanes_of(near.shape) % 2 == 1
    even_tile, odd_tile = halo_tiles(near, far, even)

    z = jnp.where(odd, got_west, got_east)
    z_east = pltpu.roll(jnp.where(odd, got_east, own_west), LANES - 1, 1)
    z_west = pltpu.roll(jnp.where(odd, own_east, got_west), 1, 1)
    lane = lanes_of((8, LANES))
    sub = lax.broadcasted_iota(jnp.int32, (8, LANES), 0)
    order = (lane + LANES - 1) % LANES

    def tile(value, index):
        return value[index * COL_TILE : (index + 1) * COL_TILE]

    def above(q):
        return jnp.where(sub == 7, pltpu.roll(pltpu.roll(q, LANES - 2, 1), 7, 0), pltpu.roll(q, 7, 0))

    def below(q):
        return jnp.where(sub == 0, pltpu.roll(pltpu.roll(q, 2, 1), 1, 0), pltpu.roll(q, 1, 0))

    zp, zp_east, zp_west = (
        packed_pressure(tile(q, COL_T), tile(q, COL_S), tile(q, COL_PS), order) for q in (z, z_east, z_west)
    )

    def centred(q):
        return q, above(q), below(q)

    def around(index):
        q = tile(z, index)
        return q, tile(z_east, index), tile(z_west, index), above(q), below(q)

    z_one = march(
        around(COL_T), around(COL_S), centred(tile(z, COL_U)), around(COL_V),
        (above(zp), below(zp)),
        (slopes(tile(z_east, COL_U), zp_east)[0], slopes(tile(z_west, COL_U), zp_west)[1]),
        tile(z, COL_WET),
        coriolis_of(8 * ((order // 2) % BLOCKS) + sub),
    )
    zp_one = packed_pressure(z_one[0], z_one[1], tile(z, COL_PS), order)

    def packed_slopes(u, p):
        to_west, to_east = slopes(u, p)
        return jnp.where(lane % 2 == 1, to_east, to_west)

    z_slopes = packed_slopes(tile(z, COL_U), zp)
    z_one_slopes = packed_slopes(z_one[2], zp_one)

    for side, block, tiles in ((0, 0, even_tile), (1, BLOCKS - 1, odd_tile)):
        psh_ref[side] = pltpu.roll(tile(tiles, COL_PS), LANES - 2 * (block + 1), 1)

    outs = (t_hbm, s_hbm, u_hbm, v_hbm, p_hbm)
    blocks = [pl.ds(8 * r, 8) for r in range(BLOCKS)]
    coriolis = [coriolis_of(8 * r + sub) for r in range(BLOCKS)]
    psv = [ps_ref[rows, :] for rows in blocks]

    def vertical(ref, lead, r, centre):
        north = ref[(*lead, pl.ds(8 * r + 1, 8))] if r < BLOCKS - 1 else pltpu.roll(centre, 7, 0)
        south = ref[(*lead, pl.ds(8 * r - 1, 8))] if r > 0 else pltpu.roll(centre, 1, 0)
        return north, south

    def level(k, running, half=0, done_ref=None, base=0):
        run0, run1, run2 = (list(x) for x in running)
        side_of = {0: 0, BLOCKS - 1: 1}
        shifts = [LANES - 2 - 8 * k - 2 * r for r in range(BLOCKS)]
        for r, rows in enumerate(blocks):
            heavy = heaviness(t_ref[k, rows, :], s_ref[k, rows, :])
            p_ref[half, rows, :] = psv[r] + GRAVITY * (run0[r] + 0.5 * heavy)
            run0[r] = run0[r] + heavy
        for r, rows in enumerate(blocks):
            tiles = odd_tile if r % 2 else even_tile
            side = side_of.get(r)

            def unpack(index):
                return pltpu.roll(tile(tiles, index), shifts[r], 1)

            def parts(index, ref):
                own, halo = ref[k, rows, :], unpack(index)
                if side is not None:
                    raw_ref[side, index, k] = own
                    rawh_ref[side, index, k] = halo
                return (own, east_of(own, halo, lane), west_of(own, halo, lane), *vertical(ref, (k,), r, own))

            p, u = p_ref[half, rows, :], u_ref[k, rows, :]
            halo = pltpu.roll(z_slopes, shifts[r], 1)
            to_west, to_east = slopes(u, p)
            wet = wet_ref[k, rows, :].astype(jnp.float32)
            if side is not None:
                raw_ref[side, 2, k] = u
                rawh_ref[side, 2, k] = unpack(COL_U)
                raw_ref[side, 4, k] = wet
                rawh_ref[side, 4, k] = unpack(COL_WET)
            new = march(
                parts(0, t_ref), parts(1, s_ref), (u, *vertical(u_ref, (k,), r, u)), parts(3, v_ref),
                vertical(p_ref, (half,), r, p),
                (east_of(to_west, halo, lane), west_of(to_east, halo, lane)),
                wet, coriolis[r],
            )
            for index in range(4):
                y_ref[half, index, rows, :] = new[index]
            heavy = heaviness(new[0], new[1])
            q_ref[half, rows, :] = psv[r] + GRAVITY * (run1[r] + 0.5 * heavy)
            run1[r] = run1[r] + heavy
        for r, rows in enumerate(blocks):
            side = side_of.get(r)

            def parts(index):
                own = y_ref[half, index, rows, :]
                halo = pltpu.roll(z_one[index], shifts[r], 1)
                if side is not None:
                    one_ref[side, index, k] = own
                    oneh_ref[side, index, k] = halo
                return (own, east_of(own, halo, lane), west_of(own, halo, lane), *vertical(y_ref, (half, index), r, own))

            p, u = q_ref[half, rows, :], y_ref[half, 2, rows, :]
            halo = pltpu.roll(z_one_slopes, shifts[r], 1)
            to_west, to_east = slopes(u, p)
            if side is not None:
                one_ref[side, 2, k] = u
                oneh_ref[side, 2, k] = pltpu.roll(z_one[2], shifts[r], 1)
            wet = wet_ref[k, rows, :].astype(jnp.float32)
            new = march(
                parts(0), parts(1), (u, *vertical(y_ref, (half, 2), r, u)), parts(3),
                vertical(q_ref, (half,), r, p),
                (east_of(to_west, halo, lane), west_of(to_east, halo, lane)),
                wet, coriolis[r],
            )
            for index in range(4):
                done_ref[index, k - base, rows, :] = new[index]
            heavy = heaviness(new[0], new[1])
            done_ref[4, k - base, rows, :] = psv[r] + GRAVITY * (run2[r] + 0.5 * heavy)
            run2[r] = run2[r] + heavy
        return tuple(tuple(x) for x in (run0, run1, run2))

    zero = tuple(jnp.zeros((8, LANES), jnp.float32) for _ in range(BLOCKS))
    running = (zero, zero, zero)
    def pair(done_ref, base):
        def run(k, running):
            running = level(2 * k, running, 0, done_ref, base)
            return level(2 * k + 1, running, 1, done_ref, base)

        return run

    for part, (first, last) in enumerate(PARTS):
        running = lax.fori_loop(first // 2, last // 2, pair(out_ref, 0), running)
        for index, out in enumerate(outs):
            levels = pl.ds(first, last - first)
            pltpu.make_async_copy(out_ref.at[index, levels], out.at[levels], sems.at[part]).start()
    lax.fori_loop(LATE // 2, LEVELS // 2, pair(late_ref, LATE), running)
    for part, (first, last) in enumerate(PARTS):
        whole = out_ref.at[:, pl.ds(first, last - first)]
        pltpu.make_async_copy(whole, whole, sems.at[part]).wait()


def patch_kernel(
    ps_ref, far_ref, near_ref, raw_ref, rawh_ref, one_ref, oneh_ref, psh_ref, late_ref, t_in, s_in, u_in, v_in, p_in,
    t_hbm, s_hbm, u_hbm, v_hbm, p_hbm, block_ref, sems,
):
    outs = (t_hbm, s_hbm, u_hbm, v_hbm, p_hbm)
    inner = pl.ds(2, ROWS - 4)
    for index, out in enumerate(outs):
        pltpu.make_async_copy(
            late_ref.at[index, :, inner], out.at[pl.ds(LATE, LEVELS - LATE), inner], sems.at[1]
        ).start()
    lat = lax.axis_index("lat")
    even = lat % 2 == 0
    lane = lanes_of((LEVELS, LANES))
    depth = lax.broadcasted_iota(jnp.int32, (LEVELS, LANES), 0)
    near, far = near_ref[...], far_ref[...]
    south = jnp.where(lat == 0, 0.0, jnp.where(even, far, near))
    north = jnp.where(even, near, far)

    def pressure(t, s, ps):
        heavy = heaviness(t, s)
        total = heavy
        for shift in (1, 2, 4, 8):
            total = total + jnp.where(depth >= shift, pltpu.roll(total, shift, 0), 0.0)
        return ps + GRAVITY * (total - 0.5 * heavy)

    def side_rows(side, value):
        rows = (0, 1, 2) if side == 0 else (7, 6, 5)
        at = [side * (ROWS - 8) + r for r in rows]
        block = BLOCKS - 1 if side == 0 else 0

        def unfold(row):
            row = jnp.broadcast_to(pltpu.roll(row, LANES - 2 * (block + 1), 1), (LEVELS, LANES))
            for bit in (1, 2, 4, 8):
                row = jnp.where(depth & bit != 0, pltpu.roll(row, LANES - 8 * bit, 1), row)
            return row

        def five(own, halo, out, inn):
            ns = (inn, out) if side == 0 else (out, inn)
            return (own, east_of(own, halo, lane), west_of(own, halo, lane), *ns)

        def five_halo(own, halo, out, inn):
            ns = (inn, out) if side == 0 else (out, inn)
            return (halo, east_of(halo, own, lane), west_of(halo, own, lane), *ns)

        ring2 = [value[(2 * i + 1) * LEVELS : (2 * i + 2) * LEVELS] for i in range(4)]
        ring1 = [value[2 * i * LEVELS : (2 * i + 1) * LEVELS] for i in range(4)]
        corner = [unfold(value[ROW_CORNER + i : ROW_CORNER + i + 1]) for i in range(5)]
        edge0 = [raw_ref[side, i, :, rows[0], :] for i in range(5)]
        edge0h = [rawh_ref[side, i, :, rows[0], :] for i in range(5)]
        edge1 = [raw_ref[side, i, :, rows[1], :] for i in range(5)]
        edge1h = [rawh_ref[side, i, :, rows[1], :] for i in range(4)]
        one1 = [one_ref[side, i, :, rows[1], :] for i in range(4)]
        one1h = [oneh_ref[side, i, :, rows[1], :] for i in range(4)]
        one2 = [one_ref[side, i, :, rows[2], :] for i in range(4)]
        wet_ring = value[ROW_WET : ROW_WET + LEVELS]
        ps_ring2, ps_ring1 = value[ROW_PS + 1 : ROW_PS + 2], value[ROW_PS : ROW_PS + 1]
        ps_corner = corner[4][0:1]
        ps0, ps1, ps2 = (ps_ref[pl.ds(a, 1), :] for a in at)
        ps0h, ps1h = (psh_ref[side, pl.ds(r, 1), :] for r in rows[:2])
        step = -1 if side == 0 else 1
        cor_ring, cor0, cor1 = (coriolis_of(jnp.int32(at[0] + d)) for d in (step, 0, -step))

        p_ring2 = pressure(ring2[0], ring2[1], ps_ring2)
        p_ring1 = pressure(ring1[0], ring1[1], ps_ring1)
        p_corner = pressure(corner[0], corner[1], ps_corner)
        p0 = pressure(edge0[0], edge0[1], ps0)
        p0h = pressure(edge0h[0], edge0h[1], ps0h)
        p1 = pressure(edge1[0], edge1[1], ps1)
        p1h = pressure(edge1h[0], edge1h[1], ps1h)

        def sides_of(u, uh, p, ph):
            west, east = slopes(u, p)
            west_halo, east_halo = slopes(uh, ph)
            return (
                (east_of(west, west_halo, lane), west_of(east, east_halo, lane)),
                (east_of(west_halo, west, lane), west_of(east_halo, east, lane)),
            )

        def ns(out, inn):
            return (inn, out) if side == 0 else (out, inn)

        sides_ring, _ = sides_of(ring1[2], corner[2], p_ring1, p_corner)
        sides0, sides0h = sides_of(edge0[2], edge0h[2], p0, p0h)
        first_ring = march(
            *(five(ring1[i], corner[i], ring2[i], edge0[i]) for i in range(2)),
            (ring1[2], *ns(ring2[2], edge0[2])),
            five(ring1[3], corner[3], ring2[3], edge0[3]),
            ns(p_ring2, p0), sides_ring, wet_ring, cor_ring,
        )
        first0 = march(
            *(five(edge0[i], edge0h[i], ring1[i], edge1[i]) for i in range(2)),
            (edge0[2], *ns(ring1[2], edge1[2])),
            five(edge0[3], edge0h[3], ring1[3], edge1[3]),
            ns(p_ring1, p1), sides0, edge0[4], cor0,
        )
        first0h = march(
            *(five_halo(edge0[i], edge0h[i], corner[i], edge1h[i]) for i in range(2)),
            (edge0h[2], *ns(corner[2], edge1h[2])),
            five_halo(edge0[3], edge0h[3], corner[3], edge1h[3]),
            ns(p_corner, p1h), sides0h, edge0h[4], cor0,
        )
        p_ring1 = pressure(first_ring[0], first_ring[1], ps_ring1)
        p0 = pressure(first0[0], first0[1], ps0)
        p0h = pressure(first0h[0], first0h[1], ps0h)
        p1 = pressure(one1[0], one1[1], ps1)
        p1h = pressure(one1h[0], one1h[1], ps1h)
        p2 = pressure(one2[0], one2[1], ps2)
        sides0, _ = sides_of(first0[2], first0h[2], p0, p0h)
        sides1, _ = sides_of(one1[2], one1h[2], p1, p1h)
        second0 = march(
            *(five(first0[i], first0h[i], first_ring[i], one1[i]) for i in range(2)),
            (first0[2], *ns(first_ring[2], one1[2])),
            five(first0[3], first0h[3], first_ring[3], one1[3]),
            ns(p_ring1, p1), sides0, edge0[4], cor0,
        )
        second1 = march(
            *(five(one1[i], one1h[i], first0[i], one2[i]) for i in range(2)),
            (one1[2], *ns(first0[2], one2[2])),
            five(one1[3], one1h[3], first0[3], one2[3]),
            ns(p0, p2), sides1, edge1[4], cor1,
        )
        second0 = (*second0, pressure(second0[0], second0[1], ps0))
        second1 = (*second1, pressure(second1[0], second1[1], ps1))
        for index, out in enumerate(outs):
            block_ref[side, index, :, side, :] = second0[index]
            block_ref[side, index, :, 1 - side, :] = second1[index]
            pltpu.make_async_copy(
                block_ref.at[side, index], out.at[:, pl.ds(side * (ROWS - 2), 2), :], sems.at[0]
            ).start()

    side_rows(0, south)
    side_rows(1, north)
    pltpu.make_async_copy(block_ref, block_ref, sems.at[0]).wait()
    whole = late_ref.at[:, :, inner]
    pltpu.make_async_copy(whole, whole, sems.at[1]).wait()


def exchanges(lon_count, lat_count):
    def at(lat, lon):
        return (lon % lon_count) * lat_count + lat

    def lat_far(lat, lon):
        if lat == 0:
            return at(0, lon ^ 1)
        if lat == lat_count - 1:
            return at(lat, lon_count - 1 - lon)
        return at(lat + 1 if lat % 2 else lat - 1, lon)

    cells = [(lat, lon) for lat in range(lat_count) for lon in range(lon_count)]
    lon_near = [(at(a, o), at(a, o ^ 1)) for a, o in cells]
    lon_far = [(at(a, o), at(a, o + 1 if o % 2 else o - 1)) for a, o in cells]
    lat_near = [(at(a, o), at(a ^ 1, o)) for a, o in cells]
    return lon_near, lon_far, lat_near, [(at(a, o), lat_far(a, o)) for a, o in cells]


def swap(value, pairs):
    return lax.ppermute(value, ("lon", "lat"), pairs)


def on_device(t, s, u, v, ps, wet):
    lon_near, lon_far, lat_near, lat_far = exchanges(lax.axis_size("lon"), lax.axis_size("lat"))
    inputs = (t, s, u, v, ps, wet)
    kept = [pltpu.with_memory_space_constraint(x, pltpu.HBM) for x in inputs]
    cols = jax.ShapeDtypeStruct((COL_ROWS, LANES), jnp.float32)
    rows = jax.ShapeDtypeStruct((ROW_ROWS, LANES), jnp.float32)

    def grant(mib):
        return pltpu.CompilerParams(vmem_limit_bytes=int(mib * 1024 * 1024))

    col_near, col_far = pl.pallas_call(
        pack_columns,
        out_shape=(cols, cols),
        in_specs=[HBM] * 6,
        out_specs=(VMEM, VMEM),
        scratch_shapes=[
            pltpu.VMEM((4, *t.shape), jnp.float32),
            pltpu.VMEM(wet.shape, wet.dtype),
            pltpu.VMEM(ps.shape, jnp.float32),
            pltpu.SemaphoreType.DMA((3,)),
        ],
        compiler_params=grant(6),
    )(*kept)
    block = (LEVELS, 8, LANES)
    row_near, row_far = pl.pallas_call(
        pack_rows,
        out_shape=(rows, rows),
        in_specs=[HBM] * 6,
        out_specs=(VMEM, VMEM),
        scratch_shapes=[
            pltpu.VMEM((2, 4, *block), jnp.float32),
            pltpu.VMEM((2, *block), jnp.int32),
            pltpu.VMEM((ROWS, LANES), jnp.float32),
            pltpu.SemaphoreType.DMA((3,)),
        ],
        compiler_params=grant(4),
    )(*kept)
    got_far = swap(col_far, lon_far)
    got_near = swap(col_near, lon_near)
    row_far, row_near = pl.pallas_call(
        pack_corners,
        out_shape=(rows, rows),
        in_specs=[VMEM] * 4,
        out_specs=(VMEM, VMEM),
        input_output_aliases={2: 0, 3: 1},
        compiler_params=grant(2),
    )(got_far, got_near, row_far, row_near)
    row_far = swap(row_far, lat_far)
    row_near = swap(row_near, lat_near)
    out = jax.ShapeDtypeStruct(t.shape, jnp.float32)

    def blocks(count):
        return jax.ShapeDtypeStruct((2, count, *block), jnp.float32)

    left = jax.ShapeDtypeStruct((5, LEVELS - LATE, ROWS, LANES), jnp.float32)
    plane = pltpu.VMEM((2, ROWS, LANES), jnp.float32)
    *outs, raw, raw_halo, one, one_halo, ps_halo, late = pl.pallas_call(
        main_kernel,
        out_shape=(out,) * 5 + (blocks(5), blocks(5), blocks(4), blocks(4), jax.ShapeDtypeStruct((2, 8, LANES), jnp.float32), left),
        in_specs=[VMEM] * 10,
        out_specs=(HBM,) * 5 + (VMEM,) * 6,
        scratch_shapes=[
            plane,
            pltpu.VMEM((2, 4, ROWS, LANES), jnp.float32),
            plane,
            pltpu.VMEM((5, *t.shape), jnp.float32),
            pltpu.SemaphoreType.DMA((len(PARTS),)),
        ],
        compiler_params=grant(12),
    )(*inputs, got_near, got_far, col_near, col_far)
    return pl.pallas_call(
        patch_kernel,
        out_shape=(out,) * 5,
        in_specs=[VMEM] * 9 + [HBM] * 5,
        out_specs=(HBM,) * 5,
        scratch_shapes=[
            pltpu.VMEM((2, 5, LEVELS, 2, LANES), jnp.float32),
            pltpu.SemaphoreType.DMA((2,)),
        ],
        input_output_aliases={9 + i: i for i in range(5)},
        compiler_params=grant(8),
    )(ps, row_far, row_near, raw, raw_halo, one, one_halo, ps_halo, late, *outs)


def solution(mesh):
    field = P(None, "lat", "lon")
    return jax.shard_map(
        on_device,
        mesh=mesh,
        in_specs=(field, field, field, field, P("lat", "lon"), field),
        out_specs=(field,) * 5,
        check_vma=False,
    )
```

```python
import jax
import jax.numpy as jnp
from jax import lax
from jax.experimental import pallas as pl
from jax.experimental.pallas import tpu as pltpu
from jax.sharding import PartitionSpec as P

STEPS = 2
HEAT_EXPANSION = 0.2
SALT_CONTRACTION = 0.15
GRAVITY = 0.5
TIME_STEP = 0.2
VISCOSITY = 0.25
DIFFUSIVITY = 0.2
ROTATION = 1.0

LEVELS = 16
ROWS = 32
LANES = 128
BLOCKS = ROWS // 8
SLOTS = LEVELS * BLOCKS

COL_T, COL_S, COL_U, COL_V, COL_WET, COL_PS = range(6)
COL_TILE = 8
COL_ROWS = 6 * COL_TILE
ROW_WET = 4 * 2 * LEVELS
ROW_PS = ROW_WET + LEVELS
ROW_CORNER = ROW_PS + 8
ROW_ROWS = ROW_CORNER + 8

PARTS = ((0, 8),)
LATE = 8

VMEM = pl.BlockSpec(memory_space=pltpu.VMEM)
HBM = pl.BlockSpec(memory_space=pltpu.HBM)


def lanes_of(shape):
    return lax.broadcasted_iota(jnp.int32, shape, len(shape) - 1)


def pack_columns(
    t_hbm, s_hbm, u_hbm, v_hbm, ps_hbm, wet_hbm, near_ref, far_ref, x_ref, wet_ref, ps_ref, sems
):
    for index, src in enumerate((t_hbm, s_hbm, u_hbm, v_hbm)):
        pltpu.make_async_copy(src, x_ref.at[index], sems.at[0]).start()
    rest = (
        pltpu.make_async_copy(wet_hbm, wet_ref, sems.at[1]),
        pltpu.make_async_copy(ps_hbm, ps_ref, sems.at[2]),
    )
    for copy in rest:
        copy.start()
    even = lax.axis_index("lon") % 2 == 0
    slot = lanes_of((8, LANES)) >> 1
    masks = [slot == j for j in range(SLOTS)]

    def pack(index, tiles):
        east = jnp.zeros((8, LANES), jnp.float32)
        west = jnp.zeros((8, LANES), jnp.float32)
        for j, tile in enumerate(tiles):
            rolled = pltpu.roll(tile(), (2 * j + 2) % LANES, 1)
            east = jnp.where(masks[j], rolled, east)
            west = jnp.where(masks[(j + 1) % SLOTS], rolled, west)
        rows = pl.ds(index * COL_TILE, COL_TILE)
        near_ref[rows, :] = jnp.where(even, east, west)
        far_ref[rows, :] = jnp.where(even, west, east)

    def tiles_of(ref):
        return [
            (lambda j=j: ref[j // BLOCKS, pl.ds(8 * (j % BLOCKS), 8), :].astype(jnp.float32))
            for j in range(SLOTS)
        ]

    pltpu.make_async_copy(x_ref, x_ref, sems.at[0]).wait()
    for index in range(4):
        pack(index, tiles_of(x_ref.at[index]))
    for copy in rest:
        copy.wait()
    pack(COL_WET, tiles_of(wet_ref))
    pack(COL_PS, [(lambda r=r: ps_ref[pl.ds(8 * r, 8), :]) for r in range(BLOCKS)])


def reverse_lanes(value):
    index = LANES - 1 - lanes_of(value.shape)
    return jnp.take_along_axis(value, index, axis=1, mode="promise_in_bounds")


def pack_rows(
    t_hbm, s_hbm, u_hbm, v_hbm, ps_hbm, wet_hbm, near_ref, far_ref, x_ref, wet_ref, ps_ref, sems
):
    rest = pltpu.make_async_copy(ps_hbm, ps_ref, sems.at[2])
    rest.start()
    for side, first in ((0, 0), (1, ROWS - 8)):
        for index, src in enumerate((t_hbm, s_hbm, u_hbm, v_hbm)):
            pltpu.make_async_copy(src.at[:, pl.ds(first, 8), :], x_ref.at[side, index], sems.at[0]).start()
        pltpu.make_async_copy(wet_hbm.at[:, pl.ds(first, 8), :], wet_ref.at[side], sems.at[1]).start()
    lat = lax.axis_index("lat")
    even = lat % 2 == 0
    fold = lat == lax.axis_size("lat") - 1
    for ref, sem in ((x_ref, 0), (wet_ref, 1)):
        pltpu.make_async_copy(ref, ref, sems.at[sem]).wait()
    rest.wait()

    def put(first, north, south, sign):
        rows = pl.ds(first, north.shape[0])
        near_ref[rows, :] = jnp.where(even, north, south)
        far_ref[rows, :] = jnp.where(even, south, north)

        @pl.when(fold)
        def _():
            far_ref[rows, :] = sign * reverse_lanes(north)

    for index, sign in enumerate((1.0, 1.0, -1.0, -1.0)):
        for ring in range(2):
            put((2 * index + ring) * LEVELS, x_ref[1, index, :, 7 - ring, :], x_ref[0, index, :, ring, :], sign)
    put(ROW_WET, wet_ref[1, :, 7, :].astype(jnp.float32), wet_ref[0, :, 0, :].astype(jnp.float32), 1.0)
    top, bottom = ps_ref[pl.ds(ROWS - 8, 8), :], ps_ref[pl.ds(0, 8), :]
    sub = lax.broadcasted_iota(jnp.int32, (8, LANES), 0)
    north = jnp.where(sub == 0, pltpu.roll(top, 1, 0), pltpu.roll(top, 3, 0))
    put(ROW_PS, north, bottom, 1.0)
    near_ref[pl.ds(ROW_CORNER, 8), :] = jnp.zeros((8, LANES), jnp.float32)
    far_ref[pl.ds(ROW_CORNER, 8), :] = jnp.zeros((8, LANES), jnp.float32)


def halo_tiles(near, far, even_lon):
    slot = lanes_of(near.shape) >> 1
    west = jnp.where(even_lon, far, near)
    east = jnp.where(even_lon, near, far)
    return (
        jnp.where(slot % 2 == 0, west, east),
        jnp.where(slot % 2 == 0, east, west),
    )


def pack_corners(far_ref, near_ref, far_in, near_in, far_out, near_out):
    lat = lax.axis_index("lat")
    even = lat % 2 == 0
    fold = lat == lax.axis_size("lat") - 1
    even_tile, odd_tile = halo_tiles(near_ref[...], far_ref[...], lax.axis_index("lon") % 2 == 0)
    lane = lanes_of((8, LANES))
    sub = lax.broadcasted_iota(jnp.int32, (8, LANES), 0)

    def gather(tile, row):
        out = jnp.zeros((8, LANES), jnp.float32)
        for index, field in enumerate((COL_T, COL_S, COL_U, COL_V, COL_PS)):
            one = pltpu.roll(tile[field * COL_TILE : (field + 1) * COL_TILE], (index - row) % 8, 0)
            out = jnp.where(sub == index, one, out)
        return out

    north, south = gather(odd_tile, 7), gather(even_tile, 0)
    mirrored = pltpu.roll(north, LANES - 6, 1)
    mirrored = jnp.where(lane % 2 == 0, pltpu.roll(mirrored, 1, 1), pltpu.roll(mirrored, LANES - 1, 1))
    mirrored = jnp.where((sub == 2) | (sub == 3), -mirrored, mirrored)
    rows = pl.ds(ROW_CORNER, 8)
    near_out[rows, :] = jnp.where(even, north, south)
    far_out[rows, :] = jnp.where(fold, mirrored, jnp.where(even, south, north))


def laplace(q):
    centre, east, west, north, south = q
    return east + west + north + south - 4.0 * centre


def slopes(u, p):
    return VISCOSITY * u - 0.5 * p, VISCOSITY * u + 0.5 * p


def march(t, s, u, v, p, sides, wet, coriolis):
    grad_y = 0.5 * (p[0] - p[1])

    def tracer(q):
        transport = -0.5 * (u[0] * (q[1] - q[2]) + v[0] * (q[3] - q[4]))
        return wet * (q[0] + TIME_STEP * (transport + DIFFUSIVITY * laplace(q)))

    push = sides[0] + sides[1] + VISCOSITY * (u[1] + u[2]) - 4.0 * VISCOSITY * u[0]
    return (
        tracer(t),
        tracer(s),
        wet * (u[0] + TIME_STEP * (coriolis * v[0] + push)),
        wet * (v[0] + TIME_STEP * (-coriolis * u[0] - grad_y + VISCOSITY * laplace(v))),
    )


def heaviness(t, s):
    return -HEAT_EXPANSION * t + SALT_CONTRACTION * s


def coriolis_of(row):
    total = ROWS * lax.axis_size("lat")
    row = jnp.minimum(lax.axis_index("lat") * ROWS + row, total - 1).astype(jnp.float32)
    return ROTATION * (2.0 * (row + 0.5) / total - 1.0)


def east_of(own, halo, lane):
    return pltpu.roll(jnp.where(lane == 0, halo, own), LANES - 1, 1)


def west_of(own, halo, lane):
    return pltpu.roll(jnp.where(lane == LANES - 1, halo, own), 1, 1)


def packed_pressure(t, s, ps, order):
    heavy = heaviness(t, s)
    total = heavy
    for shift in (8, 16, 32, 64):
        total = total + jnp.where(order >= shift, pltpu.roll(total, shift, 1), 0.0)
        ps = ps + pltpu.roll(ps, shift, 1)
    return ps + GRAVITY * (total - 0.5 * heavy)


def main_kernel(
    t_ref, s_ref, u_ref, v_ref, ps_ref, wet_ref, near_ref, far_ref, own_near_ref, own_far_ref,
    t_hbm, s_hbm, u_hbm, v_hbm, p_hbm, raw_ref, rawh_ref, one_ref, oneh_ref, two_ref, psh_ref, late_ref,
    p_ref, y_ref, q_ref, out_ref, sems,
):
    even = lax.axis_index("lon") % 2 == 0
    near, far = near_ref[...], far_ref[...]
    own_near, own_far = own_near_ref[...], own_far_ref[...]
    own_east, own_west = jnp.where(even, own_near, own_far), jnp.where(even, own_far, own_near)
    got_west, got_east = jnp.where(even, far, near), jnp.where(even, near, far)
    odd = lanes_of(near.shape) % 2 == 1

    z = jnp.where(odd, got_west, got_east)
    z_east = pltpu.roll(jnp.where(odd, got_east, own_west), LANES - 1, 1)
    z_west = pltpu.roll(jnp.where(odd, own_east, got_west), 1, 1)
    lane = lanes_of((8, LANES))
    sub = lax.broadcasted_iota(jnp.int32, (8, LANES), 0)
    order = (lane + LANES - 1) % LANES

    def tile(value, index):
        return value[index * COL_TILE : (index + 1) * COL_TILE]

    block = (order // 2) % BLOCKS

    def above(q):
        beyond = jnp.where(block == BLOCKS - 1, 0.0, pltpu.roll(pltpu.roll(q, LANES - 2, 1), 7, 0))
        return jnp.where(sub == 7, beyond, pltpu.roll(q, 7, 0))

    def below(q):
        beyond = jnp.where(block == 0, 0.0, pltpu.roll(pltpu.roll(q, 2, 1), 1, 0))
        return jnp.where(sub == 0, beyond, pltpu.roll(q, 1, 0))

    zp, zp_east, zp_west = (
        packed_pressure(tile(q, COL_T), tile(q, COL_S), tile(q, COL_PS), order) for q in (z, z_east, z_west)
    )

    def centred(q):
        return q, above(q), below(q)

    def around(index):
        q = tile(z, index)
        return q, tile(z_east, index), tile(z_west, index), above(q), below(q)

    z_one = march(
        around(COL_T), around(COL_S), centred(tile(z, COL_U)), around(COL_V),
        (above(zp), below(zp)),
        (slopes(tile(z_east, COL_U), zp_east)[0], slopes(tile(z_west, COL_U), zp_west)[1]),
        tile(z, COL_WET),
        coriolis_of(8 * block + sub),
    )
    zp_one = packed_pressure(z_one[0], z_one[1], tile(z, COL_PS), order)

    def packed_slopes(u, p):
        to_west, to_east = slopes(u, p)
        return jnp.where(lane % 2 == 1, to_east, to_west)

    z_slopes = packed_slopes(tile(z, COL_U), zp)
    z_one_slopes = packed_slopes(z_one[2], zp_one)

    for side, r in ((0, 0), (1, BLOCKS - 1)):
        psh_ref[side] = pltpu.roll(tile(z, COL_PS), LANES - 2 * (r + 1), 1)

    outs = (t_hbm, s_hbm, u_hbm, v_hbm, p_hbm)
    blocks = [pl.ds(8 * r, 8) for r in range(BLOCKS)]
    coriolis = [coriolis_of(8 * r + sub) for r in range(BLOCKS)]
    psv = [ps_ref[rows, :] for rows in blocks]

    def vertical(ref, lead, r, centre):
        north = (
            ref[(*lead, pl.ds(8 * r + 1, 8))]
            if r < BLOCKS - 1
            else jnp.where(sub == 7, 0.0, pltpu.roll(centre, 7, 0))
        )
        south = (
            ref[(*lead, pl.ds(8 * r - 1, 8))]
            if r > 0
            else jnp.where(sub == 0, 0.0, pltpu.roll(centre, 1, 0))
        )
        return north, south

    def level(k, running, half=0, done_ref=None, base=0):
        run0, run1, run2 = (list(x) for x in running)
        side_of = {0: 0, BLOCKS - 1: 1}
        shifts = [LANES - 2 - 8 * k - 2 * r for r in range(BLOCKS)]
        for r, rows in enumerate(blocks):
            heavy = heaviness(t_ref[k, rows, :], s_ref[k, rows, :])
            p_ref[half, rows, :] = psv[r] + GRAVITY * (run0[r] + 0.5 * heavy)
            run0[r] = run0[r] + heavy
        for r, rows in enumerate(blocks):
            side = side_of.get(r)

            def unpack(index):
                return pltpu.roll(tile(z, index), shifts[r], 1)

            def parts(index, ref):
                own, halo = ref[k, rows, :], unpack(index)
                if side is not None:
                    raw_ref[side, index, k] = own
                    if index == 3:
                        rawh_ref[side, 0, k] = halo
                return (own, east_of(own, halo, lane), west_of(own, halo, lane), *vertical(ref, (k,), r, own))

            p, u = p_ref[half, rows, :], u_ref[k, rows, :]
            halo = pltpu.roll(z_slopes, shifts[r], 1)
            to_west, to_east = slopes(u, p)
            wet = wet_ref[k, rows, :].astype(jnp.float32)
            if side is not None:
                raw_ref[side, 2, k] = u
                raw_ref[side, 4, k] = wet
                raw_ref[side, 5, k] = p
                rawh_ref[side, 1, k] = unpack(COL_WET)
            new = march(
                parts(0, t_ref), parts(1, s_ref), (u, *vertical(u_ref, (k,), r, u)), parts(3, v_ref),
                vertical(p_ref, (half,), r, p),
                (east_of(to_west, halo, lane), west_of(to_east, halo, lane)),
                wet, coriolis[r],
            )
            for index in range(4):
                y_ref[half, index, rows, :] = new[index]
            heavy = heaviness(new[0], new[1])
            q_ref[half, rows, :] = psv[r] + GRAVITY * (run1[r] + 0.5 * heavy)
            run1[r] = run1[r] + heavy
        for r, rows in enumerate(blocks):
            side = side_of.get(r)

            def parts(index):
                own = y_ref[half, index, rows, :]
                halo = pltpu.roll(z_one[index], shifts[r], 1)
                if side is not None:
                    one_ref[side, index, k] = own
                    oneh_ref[side, index, k] = halo
                return (own, east_of(own, halo, lane), west_of(own, halo, lane), *vertical(y_ref, (half, index), r, own))

            p, u = q_ref[half, rows, :], y_ref[half, 2, rows, :]
            halo = pltpu.roll(z_one_slopes, shifts[r], 1)
            to_west, to_east = slopes(u, p)
            if side is not None:
                one_ref[side, 2, k] = u
                one_ref[side, 4, k] = p
                oneh_ref[side, 2, k] = pltpu.roll(z_one[2], shifts[r], 1)
            wet = wet_ref[k, rows, :].astype(jnp.float32)
            new = march(
                parts(0), parts(1), (u, *vertical(y_ref, (half, 2), r, u)), parts(3),
                vertical(q_ref, (half,), r, p),
                (east_of(to_west, halo, lane), west_of(to_east, halo, lane)),
                wet, coriolis[r],
            )
            for index in range(4):
                done_ref[index, k - base, rows, :] = new[index]
                if side is not None:
                    two_ref[side, index, k] = new[index]
            heavy = heaviness(new[0], new[1])
            done_ref[4, k - base, rows, :] = psv[r] + GRAVITY * (run2[r] + 0.5 * heavy)
            run2[r] = run2[r] + heavy
        return tuple(tuple(x) for x in (run0, run1, run2))

    zero = tuple(jnp.zeros((8, LANES), jnp.float32) for _ in range(BLOCKS))
    running = (zero, zero, zero)
    def pair(done_ref, base):
        def run(k, running):
            running = level(2 * k, running, 0, done_ref, base)
            return level(2 * k + 1, running, 1, done_ref, base)

        return run

    for part, (first, last) in enumerate(PARTS):
        running = lax.fori_loop(first // 2, last // 2, pair(out_ref, 0), running)
        for index, out in enumerate(outs):
            levels = pl.ds(first, last - first)
            pltpu.make_async_copy(out_ref.at[index, levels], out.at[levels], sems.at[part]).start()
    lax.fori_loop(LATE // 2, LEVELS // 2, pair(late_ref, LATE), running)
    for part, (first, last) in enumerate(PARTS):
        whole = out_ref.at[:, pl.ds(first, last - first)]
        pltpu.make_async_copy(whole, whole, sems.at[part]).wait()


def patch_kernel(
    ps_ref, far_ref, near_ref, raw_ref, rawh_ref, one_ref, oneh_ref, two_ref, psh_ref, late_ref, t_in, s_in, u_in, v_in, p_in,
    t_hbm, s_hbm, u_hbm, v_hbm, p_hbm, block_ref, sems,
):
    outs = (t_hbm, s_hbm, u_hbm, v_hbm, p_hbm)
    inner = pl.ds(2, ROWS - 4)
    for index, out in enumerate(outs):
        pltpu.make_async_copy(
            late_ref.at[index, :, inner], out.at[pl.ds(LATE, LEVELS - LATE), inner], sems.at[1]
        ).start()
    lat = lax.axis_index("lat")
    even = lat % 2 == 0
    lane = lanes_of((LEVELS, LANES))
    depth = lax.broadcasted_iota(jnp.int32, (LEVELS, LANES), 0)
    near, far = near_ref[...], far_ref[...]
    south = jnp.where(lat == 0, 0.0, jnp.where(even, far, near))
    north = jnp.where(even, near, far)

    def pressure(t, s, ps):
        heavy = heaviness(t, s)
        total = heavy
        for shift in (1, 2, 4, 8):
            total = total + jnp.where(depth >= shift, pltpu.roll(total, shift, 0), 0.0)
        return ps + GRAVITY * (total - 0.5 * heavy)

    def side_rows(side, value):
        row0, row1 = (0, 1) if side == 0 else (7, 6)
        first = side * (ROWS - 8)
        block = BLOCKS - 1 if side == 0 else 0
        toward = 0.5 if side == 0 else -0.5

        def unfold(row):
            row = jnp.broadcast_to(pltpu.roll(row, LANES - 2 * (block + 1), 1), (LEVELS, LANES))
            for bit in (1, 2, 4, 8):
                row = jnp.where(depth & bit != 0, pltpu.roll(row, LANES - 8 * bit, 1), row)
            return row

        def ns(out, inn):
            return (inn, out) if side == 0 else (out, inn)

        def five(own, halo, out, inn):
            return (own, east_of(own, halo, lane), west_of(own, halo, lane), *ns(out, inn))

        def sides_of(u, uh, p, ph):
            west, east = slopes(u, p)
            west_halo, east_halo = slopes(uh, ph)
            return east_of(west, west_halo, lane), west_of(east, east_halo, lane)

        def share(v, wet, beyond, p):
            wet = TIME_STEP * wet
            weight = wet * (DIFFUSIVITY + toward * v)
            return (
                weight * beyond[0],
                weight * beyond[1],
                wet * (VISCOSITY * beyond[2]),
                wet * (VISCOSITY * beyond[3] + toward * p),
            )

        def plus(a, b):
            return [x + y for x, y in zip(a, b)]

        ring2 = [value[(2 * i + 1) * LEVELS : (2 * i + 2) * LEVELS] for i in range(4)]
        ring1 = [value[2 * i * LEVELS : (2 * i + 1) * LEVELS] for i in range(4)]
        corner = [unfold(value[ROW_CORNER + i : ROW_CORNER + i + 1]) for i in range(5)]
        edge = [raw_ref[side, i, :, row0, :] for i in range(4)]
        wet0, wet1 = raw_ref[side, 4, :, row0, :], raw_ref[side, 4, :, row1, :]
        p_edge = raw_ref[side, 5, :, row0, :]
        v_halo, wet_halo = (rawh_ref[side, i, :, row0, :] for i in range(2))
        one1 = [one_ref[side, i, :, row1, :] for i in range(4)]
        p_one1 = one_ref[side, 4, :, row1, :]
        wet_ring = value[ROW_WET : ROW_WET + LEVELS]
        ps_ring2, ps_ring1 = value[ROW_PS + 1 : ROW_PS + 2], value[ROW_PS : ROW_PS + 1]
        ps0, ps1 = (ps_ref[pl.ds(first + row, 1), :] for row in (row0, row1))
        ps_halo = psh_ref[side, pl.ds(row0, 1), :]
        cor0 = coriolis_of(jnp.int32(first + row0))
        cor_ring = coriolis_of(jnp.int32(first + row0 + (-1 if side == 0 else 1)))

        p_ring2 = pressure(ring2[0], ring2[1], ps_ring2)
        p_ring1 = pressure(ring1[0], ring1[1], ps_ring1)
        p_corner = pressure(corner[0], corner[1], corner[4][0:1])
        ring = march(
            *(five(ring1[i], corner[i], ring2[i], edge[i]) for i in range(2)),
            (ring1[2], *ns(ring2[2], edge[2])),
            five(ring1[3], corner[3], ring2[3], edge[3]),
            ns(p_ring2, p_edge),
            sides_of(ring1[2], corner[2], p_ring1, p_corner),
            wet_ring, cor_ring,
        )
        added = share(edge[3], wet0, ring1, p_ring1)
        one0 = plus([one_ref[side, i, :, row0, :] for i in range(4)], added)
        one0h = plus(
            [oneh_ref[side, i, :, row0, :] for i in range(4)], share(v_halo, wet_halo, corner, p_corner)
        )
        second0 = march(
            *(five(one0[i], one0h[i], ring[i], one1[i]) for i in range(2)),
            (one0[2], *ns(ring[2], one1[2])),
            five(one0[3], one0h[3], ring[3], one1[3]),
            ns(pressure(ring[0], ring[1], ps_ring1), p_one1),
            sides_of(one0[2], one0h[2], pressure(one0[0], one0[1], ps0), pressure(one0h[0], one0h[1], ps_halo)),
            wet0, cor0,
        )
        second1 = plus(
            [two_ref[side, i, :, row1, :] for i in range(4)],
            share(one1[3], wet1, added, pressure(added[0], added[1], 0.0)),
        )
        second0 = (*second0, pressure(second0[0], second0[1], ps0))
        second1 = (*second1, pressure(second1[0], second1[1], ps1))
        for index, out in enumerate(outs):
            block_ref[side, index, :, side, :] = second0[index]
            block_ref[side, index, :, 1 - side, :] = second1[index]
            pltpu.make_async_copy(
                block_ref.at[side, index], out.at[:, pl.ds(side * (ROWS - 2), 2), :], sems.at[0]
            ).start()

    side_rows(0, south)
    side_rows(1, north)
    pltpu.make_async_copy(block_ref, block_ref, sems.at[0]).wait()
    whole = late_ref.at[:, :, inner]
    pltpu.make_async_copy(whole, whole, sems.at[1]).wait()


def exchanges(lon_count, lat_count):
    def at(lat, lon):
        return (lon % lon_count) * lat_count + lat

    def lat_far(lat, lon):
        if lat == 0:
            return at(0, lon ^ 1)
        if lat == lat_count - 1:
            return at(lat, lon_count - 1 - lon)
        return at(lat + 1 if lat % 2 else lat - 1, lon)

    cells = [(lat, lon) for lat in range(lat_count) for lon in range(lon_count)]
    lon_near = [(at(a, o), at(a, o ^ 1)) for a, o in cells]
    lon_far = [(at(a, o), at(a, o + 1 if o % 2 else o - 1)) for a, o in cells]
    lat_near = [(at(a, o), at(a ^ 1, o)) for a, o in cells]
    return lon_near, lon_far, lat_near, [(at(a, o), lat_far(a, o)) for a, o in cells]


def swap(value, pairs):
    return lax.ppermute(value, ("lon", "lat"), pairs)


def on_device(t, s, u, v, ps, wet):
    lon_near, lon_far, lat_near, lat_far = exchanges(lax.axis_size("lon"), lax.axis_size("lat"))
    inputs = (t, s, u, v, ps, wet)
    kept = [pltpu.with_memory_space_constraint(x, pltpu.HBM) for x in inputs]
    cols = jax.ShapeDtypeStruct((COL_ROWS, LANES), jnp.float32)
    rows = jax.ShapeDtypeStruct((ROW_ROWS, LANES), jnp.float32)

    def grant(mib):
        return pltpu.CompilerParams(vmem_limit_bytes=int(mib * 1024 * 1024))

    col_near, col_far = pl.pallas_call(
        pack_columns,
        out_shape=(cols, cols),
        in_specs=[HBM] * 6,
        out_specs=(VMEM, VMEM),
        scratch_shapes=[
            pltpu.VMEM((4, *t.shape), jnp.float32),
            pltpu.VMEM(wet.shape, wet.dtype),
            pltpu.VMEM(ps.shape, jnp.float32),
            pltpu.SemaphoreType.DMA((3,)),
        ],
        compiler_params=grant(6),
    )(*kept)
    block = (LEVELS, 8, LANES)
    row_near, row_far = pl.pallas_call(
        pack_rows,
        out_shape=(rows, rows),
        in_specs=[HBM] * 6,
        out_specs=(VMEM, VMEM),
        scratch_shapes=[
            pltpu.VMEM((2, 4, *block), jnp.float32),
            pltpu.VMEM((2, *block), jnp.int32),
            pltpu.VMEM((ROWS, LANES), jnp.float32),
            pltpu.SemaphoreType.DMA((3,)),
        ],
        compiler_params=grant(4),
    )(*kept)
    got_far = swap(col_far, lon_far)
    got_near = swap(col_near, lon_near)
    row_far, row_near = pl.pallas_call(
        pack_corners,
        out_shape=(rows, rows),
        in_specs=[VMEM] * 4,
        out_specs=(VMEM, VMEM),
        input_output_aliases={2: 0, 3: 1},
        compiler_params=grant(2),
    )(got_far, got_near, row_far, row_near)
    row_far = swap(row_far, lat_far)
    row_near = swap(row_near, lat_near)
    out = jax.ShapeDtypeStruct(t.shape, jnp.float32)

    def blocks(count):
        return jax.ShapeDtypeStruct((2, count, *block), jnp.float32)

    left = jax.ShapeDtypeStruct((5, LEVELS - LATE, ROWS, LANES), jnp.float32)
    plane = pltpu.VMEM((2, ROWS, LANES), jnp.float32)
    *outs, raw, raw_halo, one, one_halo, two, ps_halo, late = pl.pallas_call(
        main_kernel,
        out_shape=(out,) * 5 + (blocks(6), blocks(2), blocks(5), blocks(4), blocks(4), jax.ShapeDtypeStruct((2, 8, LANES), jnp.float32), left),
        in_specs=[VMEM] * 10,
        out_specs=(HBM,) * 5 + (VMEM,) * 7,
        scratch_shapes=[
            plane,
            pltpu.VMEM((2, 4, ROWS, LANES), jnp.float32),
            plane,
            pltpu.VMEM((5, *t.shape), jnp.float32),
            pltpu.SemaphoreType.DMA((len(PARTS),)),
        ],
        compiler_params=grant(12),
    )(*inputs, got_near, got_far, col_near, col_far)
    return pl.pallas_call(
        patch_kernel,
        out_shape=(out,) * 5,
        in_specs=[VMEM] * 10 + [HBM] * 5,
        out_specs=(HBM,) * 5,
        scratch_shapes=[
            pltpu.VMEM((2, 5, LEVELS, 2, LANES), jnp.float32),
            pltpu.SemaphoreType.DMA((2,)),
        ],
        input_output_aliases={10 + i: i for i in range(5)},
        compiler_params=grant(8),
    )(ps, row_far, row_near, raw, raw_halo, one, one_halo, two, ps_halo, late, *outs)


def solution(mesh):
    field = P(None, "lat", "lon")
    return jax.shard_map(
        on_device,
        mesh=mesh,
        in_specs=(field, field, field, field, P("lat", "lon"), field),
        out_specs=(field,) * 5,
        check_vma=False,
    )
```

```python
import jax
import jax.numpy as jnp
from jax import lax
from jax.experimental import pallas as pl
from jax.experimental.pallas import tpu as pltpu
from jax.sharding import PartitionSpec as P

STEPS = 2
HEAT_EXPANSION = 0.2
SALT_CONTRACTION = 0.15
GRAVITY = 0.5
TIME_STEP = 0.2
VISCOSITY = 0.25
DIFFUSIVITY = 0.2
ROTATION = 1.0

LEVELS = 16
ROWS = 32
LANES = 128
BLOCKS = ROWS // 8
SLOTS = LEVELS * BLOCKS

COL_T, COL_S, COL_U, COL_V, COL_WET, COL_PS = range(6)
COL_TILE = 8
COL_ROWS = 6 * COL_TILE
ROW_WET = 4 * 2 * LEVELS
ROW_PS = ROW_WET + LEVELS
ROW_CORNER = ROW_PS + 8
ROW_ROWS = ROW_CORNER + 8

PARTS = ((0, 10),)
LATE = 10

VMEM = pl.BlockSpec(memory_space=pltpu.VMEM)
HBM = pl.BlockSpec(memory_space=pltpu.HBM)


def lanes_of(shape):
    return lax.broadcasted_iota(jnp.int32, shape, len(shape) - 1)


def pack_columns(
    t_hbm, s_hbm, u_hbm, v_hbm, ps_hbm, wet_hbm, near_ref, far_ref, x_ref, wet_ref, ps_ref, sems
):
    for index, src in enumerate((t_hbm, s_hbm, u_hbm, v_hbm)):
        pltpu.make_async_copy(src, x_ref.at[index], sems.at[0]).start()
    rest = (
        pltpu.make_async_copy(wet_hbm, wet_ref, sems.at[1]),
        pltpu.make_async_copy(ps_hbm, ps_ref, sems.at[2]),
    )
    for copy in rest:
        copy.start()
    even = lax.axis_index("lon") % 2 == 0
    slot = lanes_of((8, LANES)) >> 1
    pair = slot >> 1
    odd_pair = ((slot + SLOTS - 1) & (SLOTS - 1)) >> 1
    split = slot & 1 == 0

    def pack(index, tiles):
        merged = [jnp.zeros((8, LANES), jnp.float32)] * 2
        for j, tile in enumerate(tiles):
            rolled = pltpu.roll(tile(), (2 * j + 2) % LANES, 1)
            merged[j % 2] = jnp.where((odd_pair if j % 2 else pair) == j // 2, rolled, merged[j % 2])
        east = jnp.where(split, merged[0], merged[1])
        west = jnp.where(split, merged[1], merged[0])
        rows = pl.ds(index * COL_TILE, COL_TILE)
        near_ref[rows, :] = jnp.where(even, east, west)
        far_ref[rows, :] = jnp.where(even, west, east)

    def tiles_of(ref):
        return [
            (lambda j=j: ref[j // BLOCKS, pl.ds(8 * (j % BLOCKS), 8), :].astype(jnp.float32))
            for j in range(SLOTS)
        ]

    pltpu.make_async_copy(x_ref, x_ref, sems.at[0]).wait()
    for index in range(4):
        pack(index, tiles_of(x_ref.at[index]))
    for copy in rest:
        copy.wait()
    pack(COL_WET, tiles_of(wet_ref))
    pack(COL_PS, [(lambda r=r: ps_ref[pl.ds(8 * r, 8), :]) for r in range(BLOCKS)])


def reverse_lanes(value):
    index = LANES - 1 - lanes_of(value.shape)
    return jnp.take_along_axis(value, index, axis=1, mode="promise_in_bounds")


def pack_rows(
    t_hbm, s_hbm, u_hbm, v_hbm, ps_hbm, wet_hbm, near_ref, far_ref, x_ref, wet_ref, ps_ref, sems
):
    rest = pltpu.make_async_copy(ps_hbm, ps_ref, sems.at[2])
    rest.start()
    for side, first in ((0, 0), (1, ROWS - 8)):
        for index, src in enumerate((t_hbm, s_hbm, u_hbm, v_hbm)):
            pltpu.make_async_copy(src.at[:, pl.ds(first, 8), :], x_ref.at[side, index], sems.at[0]).start()
        pltpu.make_async_copy(wet_hbm.at[:, pl.ds(first, 8), :], wet_ref.at[side], sems.at[1]).start()
    lat = lax.axis_index("lat")
    even = lat % 2 == 0
    fold = lat == lax.axis_size("lat") - 1
    for ref, sem in ((x_ref, 0), (wet_ref, 1)):
        pltpu.make_async_copy(ref, ref, sems.at[sem]).wait()
    rest.wait()

    def put(first, north, south, sign):
        rows = pl.ds(first, north.shape[0])
        near_ref[rows, :] = jnp.where(even, north, south)
        far_ref[rows, :] = jnp.where(even, south, north)

        @pl.when(fold)
        def _():
            far_ref[rows, :] = sign * reverse_lanes(north)

    for index, sign in enumerate((1.0, 1.0, -1.0, -1.0)):
        for ring in range(2):
            put((2 * index + ring) * LEVELS, x_ref[1, index, :, 7 - ring, :], x_ref[0, index, :, ring, :], sign)
    put(ROW_WET, wet_ref[1, :, 7, :].astype(jnp.float32), wet_ref[0, :, 0, :].astype(jnp.float32), 1.0)
    top, bottom = ps_ref[pl.ds(ROWS - 8, 8), :], ps_ref[pl.ds(0, 8), :]
    sub = lax.broadcasted_iota(jnp.int32, (8, LANES), 0)
    north = jnp.where(sub == 0, pltpu.roll(top, 1, 0), pltpu.roll(top, 3, 0))
    put(ROW_PS, north, bottom, 1.0)
    near_ref[pl.ds(ROW_CORNER, 8), :] = jnp.zeros((8, LANES), jnp.float32)
    far_ref[pl.ds(ROW_CORNER, 8), :] = jnp.zeros((8, LANES), jnp.float32)


def halo_tiles(near, far, even_lon):
    slot = lanes_of(near.shape) >> 1
    west = jnp.where(even_lon, far, near)
    east = jnp.where(even_lon, near, far)
    return (
        jnp.where(slot % 2 == 0, west, east),
        jnp.where(slot % 2 == 0, east, west),
    )


def pack_corners(far_ref, near_ref, far_in, near_in, far_out, near_out):
    lat = lax.axis_index("lat")
    even = lat % 2 == 0
    fold = lat == lax.axis_size("lat") - 1
    even_tile, odd_tile = halo_tiles(near_ref[...], far_ref[...], lax.axis_index("lon") % 2 == 0)
    lane = lanes_of((8, LANES))
    sub = lax.broadcasted_iota(jnp.int32, (8, LANES), 0)

    def gather(tile, row):
        out = jnp.zeros((8, LANES), jnp.float32)
        for index, field in enumerate((COL_T, COL_S, COL_U, COL_V, COL_PS)):
            one = pltpu.roll(tile[field * COL_TILE : (field + 1) * COL_TILE], (index - row) % 8, 0)
            out = jnp.where(sub == index, one, out)
        return out

    north, south = gather(odd_tile, 7), gather(even_tile, 0)
    mirrored = pltpu.roll(north, LANES - 6, 1)
    mirrored = jnp.where(lane % 2 == 0, pltpu.roll(mirrored, 1, 1), pltpu.roll(mirrored, LANES - 1, 1))
    mirrored = jnp.where((sub == 2) | (sub == 3), -mirrored, mirrored)
    rows = pl.ds(ROW_CORNER, 8)
    near_out[rows, :] = jnp.where(even, north, south)
    far_out[rows, :] = jnp.where(fold, mirrored, jnp.where(even, south, north))


def laplace(q):
    centre, east, west, north, south = q
    return east + west + north + south - 4.0 * centre


def slopes(u, p):
    return VISCOSITY * u - 0.5 * p, VISCOSITY * u + 0.5 * p


def march(t, s, u, v, p, sides, wet, coriolis):
    grad_y = 0.5 * (p[0] - p[1])

    def tracer(q):
        transport = -0.5 * (u[0] * (q[1] - q[2]) + v[0] * (q[3] - q[4]))
        return wet * (q[0] + TIME_STEP * (transport + DIFFUSIVITY * laplace(q)))

    push = sides[0] + sides[1] + VISCOSITY * (u[1] + u[2]) - 4.0 * VISCOSITY * u[0]
    return (
        tracer(t),
        tracer(s),
        wet * (u[0] + TIME_STEP * (coriolis * v[0] + push)),
        wet * (v[0] + TIME_STEP * (-coriolis * u[0] - grad_y + VISCOSITY * laplace(v))),
    )


def heaviness(t, s):
    return -HEAT_EXPANSION * t + SALT_CONTRACTION * s


def coriolis_of(row):
    total = ROWS * lax.axis_size("lat")
    row = jnp.minimum(lax.axis_index("lat") * ROWS + row, total - 1).astype(jnp.float32)
    return ROTATION * (2.0 * (row + 0.5) / total - 1.0)


def east_of(own, halo, lane):
    return pltpu.roll(jnp.where(lane == 0, halo, own), LANES - 1, 1)


def west_of(own, halo, lane):
    return pltpu.roll(jnp.where(lane == LANES - 1, halo, own), 1, 1)


def packed_pressure(t, s, ps, order):
    heavy = heaviness(t, s)
    total = heavy
    for shift in (8, 16, 32, 64):
        total = total + jnp.where(order >= shift, pltpu.roll(total, shift, 1), 0.0)
        ps = ps + pltpu.roll(ps, shift, 1)
    return ps + GRAVITY * (total - 0.5 * heavy)


def main_kernel(
    t_ref, s_ref, u_ref, v_ref, ps_ref, wet_ref, near_ref, far_ref, own_near_ref, own_far_ref,
    t_hbm, s_hbm, u_hbm, v_hbm, p_hbm, raw_ref, rawh_ref, one_ref, oneh_ref, two_ref, psh_ref, late_ref,
    p_ref, y_ref, q_ref, out_ref, sems,
):
    even = lax.axis_index("lon") % 2 == 0
    near, far = near_ref[...], far_ref[...]
    own_near, own_far = own_near_ref[...], own_far_ref[...]
    own_east, own_west = jnp.where(even, own_near, own_far), jnp.where(even, own_far, own_near)
    got_west, got_east = jnp.where(even, far, near), jnp.where(even, near, far)
    odd = lanes_of(near.shape) % 2 == 1

    z = jnp.where(odd, got_west, got_east)
    z_east = pltpu.roll(jnp.where(odd, got_east, own_west), LANES - 1, 1)
    z_west = pltpu.roll(jnp.where(odd, own_east, got_west), 1, 1)
    lane = lanes_of((8, LANES))
    sub = lax.broadcasted_iota(jnp.int32, (8, LANES), 0)
    order = (lane + LANES - 1) % LANES

    def tile(value, index):
        return value[index * COL_TILE : (index + 1) * COL_TILE]

    block = (order // 2) % BLOCKS

    def above(q):
        beyond = jnp.where(block == BLOCKS - 1, 0.0, pltpu.roll(pltpu.roll(q, LANES - 2, 1), 7, 0))
        return jnp.where(sub == 7, beyond, pltpu.roll(q, 7, 0))

    def below(q):
        beyond = jnp.where(block == 0, 0.0, pltpu.roll(pltpu.roll(q, 2, 1), 1, 0))
        return jnp.where(sub == 0, beyond, pltpu.roll(q, 1, 0))

    zp, zp_east, zp_west = (
        packed_pressure(tile(q, COL_T), tile(q, COL_S), tile(q, COL_PS), order) for q in (z, z_east, z_west)
    )

    def centred(q):
        return q, above(q), below(q)

    def around(index):
        q = tile(z, index)
        return q, tile(z_east, index), tile(z_west, index), above(q), below(q)

    z_one = march(
        around(COL_T), around(COL_S), centred(tile(z, COL_U)), around(COL_V),
        (above(zp), below(zp)),
        (slopes(tile(z_east, COL_U), zp_east)[0], slopes(tile(z_west, COL_U), zp_west)[1]),
        tile(z, COL_WET),
        coriolis_of(8 * block + sub),
    )
    zp_one = packed_pressure(z_one[0], z_one[1], tile(z, COL_PS), order)

    def packed_slopes(u, p):
        to_west, to_east = slopes(u, p)
        return jnp.where(lane % 2 == 1, to_east, to_west)

    z_slopes = packed_slopes(tile(z, COL_U), zp)
    z_one_slopes = packed_slopes(z_one[2], zp_one)

    for side, r in ((0, 0), (1, BLOCKS - 1)):
        psh_ref[side] = pltpu.roll(tile(z, COL_PS), LANES - 2 * (r + 1), 1)

    outs = (t_hbm, s_hbm, u_hbm, v_hbm, p_hbm)
    blocks = [pl.ds(8 * r, 8) for r in range(BLOCKS)]
    coriolis = [coriolis_of(8 * r + sub) for r in range(BLOCKS)]
    psv = [ps_ref[rows, :] for rows in blocks]

    padded = [pl.ds(8 * r + 8, 8) for r in range(BLOCKS)]
    blank = jnp.zeros((8, LANES), jnp.float32)
    for half in range(2):
        for pad in (pl.ds(0, 8), pl.ds(ROWS + 8, 8)):
            p_ref[half, pad, :] = blank
            q_ref[half, pad, :] = blank
            for index in range(4):
                y_ref[half, index, pad, :] = blank

    def beside(ref, lead, r):
        return ref[(*lead, pl.ds(8 * r + 9, 8))], ref[(*lead, pl.ds(8 * r + 7, 8))]

    def vertical(ref, lead, r, centre):
        north = (
            ref[(*lead, pl.ds(8 * r + 1, 8))]
            if r < BLOCKS - 1
            else jnp.where(sub == 7, 0.0, pltpu.roll(centre, 7, 0))
        )
        south = (
            ref[(*lead, pl.ds(8 * r - 1, 8))]
            if r > 0
            else jnp.where(sub == 0, 0.0, pltpu.roll(centre, 1, 0))
        )
        return north, south

    def level(k, running, half=0, done_ref=None, base=0):
        run0, run1, run2 = (list(x) for x in running)
        side_of = {0: 0, BLOCKS - 1: 1}
        shifts = [LANES - 2 - 8 * k - 2 * r for r in range(BLOCKS)]
        for r, rows in enumerate(blocks):
            heavy = heaviness(t_ref[k, rows, :], s_ref[k, rows, :])
            p_ref[half, padded[r], :] = psv[r] + GRAVITY * (run0[r] + 0.5 * heavy)
            run0[r] = run0[r] + heavy
        for r, rows in enumerate(blocks):
            side = side_of.get(r)

            def unpack(index):
                return pltpu.roll(tile(z, index), shifts[r], 1)

            def parts(index, ref):
                own, halo = ref[k, rows, :], unpack(index)
                if side is not None:
                    raw_ref[side, index, k] = own
                    if index == 3:
                        rawh_ref[side, 0, k] = halo
                return (own, east_of(own, halo, lane), west_of(own, halo, lane), *vertical(ref, (k,), r, own))

            p, u = p_ref[half, padded[r], :], u_ref[k, rows, :]
            halo = pltpu.roll(z_slopes, shifts[r], 1)
            to_west, to_east = slopes(u, p)
            wet = wet_ref[k, rows, :].astype(jnp.float32)
            if side is not None:
                raw_ref[side, 2, k] = u
                raw_ref[side, 4, k] = wet
                raw_ref[side, 5, k] = p
                rawh_ref[side, 1, k] = unpack(COL_WET)
            new = march(
                parts(0, t_ref), parts(1, s_ref), (u, *vertical(u_ref, (k,), r, u)), parts(3, v_ref),
                beside(p_ref, (half,), r),
                (east_of(to_west, halo, lane), west_of(to_east, halo, lane)),
                wet, coriolis[r],
            )
            for index in range(4):
                y_ref[half, index, padded[r], :] = new[index]
            heavy = heaviness(new[0], new[1])
            q_ref[half, padded[r], :] = psv[r] + GRAVITY * (run1[r] + 0.5 * heavy)
            run1[r] = run1[r] + heavy
        for r, rows in enumerate(blocks):
            side = side_of.get(r)

            def parts(index):
                own = y_ref[half, index, padded[r], :]
                halo = pltpu.roll(z_one[index], shifts[r], 1)
                if side is not None:
                    one_ref[side, index, k] = own
                    oneh_ref[side, index, k] = halo
                return (own, east_of(own, halo, lane), west_of(own, halo, lane), *beside(y_ref, (half, index), r))

            p, u = q_ref[half, padded[r], :], y_ref[half, 2, padded[r], :]
            halo = pltpu.roll(z_one_slopes, shifts[r], 1)
            to_west, to_east = slopes(u, p)
            if side is not None:
                one_ref[side, 2, k] = u
                one_ref[side, 4, k] = p
                oneh_ref[side, 2, k] = pltpu.roll(z_one[2], shifts[r], 1)
            wet = wet_ref[k, rows, :].astype(jnp.float32)
            new = march(
                parts(0), parts(1), (u, *beside(y_ref, (half, 2), r)), parts(3),
                beside(q_ref, (half,), r),
                (east_of(to_west, halo, lane), west_of(to_east, halo, lane)),
                wet, coriolis[r],
            )
            for index in range(4):
                done_ref[index, k - base, rows, :] = new[index]
                if side is not None:
                    two_ref[side, index, k] = new[index]
            heavy = heaviness(new[0], new[1])
            done_ref[4, k - base, rows, :] = psv[r] + GRAVITY * (run2[r] + 0.5 * heavy)
            run2[r] = run2[r] + heavy
        return tuple(tuple(x) for x in (run0, run1, run2))

    zero = tuple(jnp.zeros((8, LANES), jnp.float32) for _ in range(BLOCKS))
    running = (zero, zero, zero)
    def pair(done_ref, base):
        def run(k, running):
            running = level(2 * k, running, 0, done_ref, base)
            return level(2 * k + 1, running, 1, done_ref, base)

        return run

    for part, (first, last) in enumerate(PARTS):
        running = lax.fori_loop(first // 2, last // 2, pair(out_ref, 0), running)
        for index, out in enumerate(outs):
            levels = pl.ds(first, last - first)
            pltpu.make_async_copy(out_ref.at[index, levels], out.at[levels], sems.at[part]).start()
    lax.fori_loop(LATE // 2, LEVELS // 2, pair(late_ref, LATE), running)
    for part, (first, last) in enumerate(PARTS):
        whole = out_ref.at[:, pl.ds(first, last - first)]
        pltpu.make_async_copy(whole, whole, sems.at[part]).wait()


def patch_kernel(
    ps_ref, far_ref, near_ref, raw_ref, rawh_ref, one_ref, oneh_ref, two_ref, psh_ref, late_ref, t_in, s_in, u_in, v_in, p_in,
    t_hbm, s_hbm, u_hbm, v_hbm, p_hbm, block_ref, sems,
):
    outs = (t_hbm, s_hbm, u_hbm, v_hbm, p_hbm)
    inner = pl.ds(2, ROWS - 4)
    for index, out in enumerate(outs):
        pltpu.make_async_copy(
            late_ref.at[index, :, inner], out.at[pl.ds(LATE, LEVELS - LATE), inner], sems.at[1]
        ).start()
    lat = lax.axis_index("lat")
    even = lat % 2 == 0
    lane = lanes_of((LEVELS, LANES))
    depth = lax.broadcasted_iota(jnp.int32, (LEVELS, LANES), 0)
    near, far = near_ref[...], far_ref[...]
    south = jnp.where(lat == 0, 0.0, jnp.where(even, far, near))
    north = jnp.where(even, near, far)

    def pressure(t, s, ps):
        heavy = heaviness(t, s)
        total = heavy
        for shift in (1, 2, 4, 8):
            total = total + jnp.where(depth >= shift, pltpu.roll(total, shift, 0), 0.0)
        return ps + GRAVITY * (total - 0.5 * heavy)

    def side_rows(side, value):
        row0, row1 = (0, 1) if side == 0 else (7, 6)
        first = side * (ROWS - 8)
        block = BLOCKS - 1 if side == 0 else 0
        toward = 0.5 if side == 0 else -0.5

        def unfold(row):
            row = jnp.broadcast_to(pltpu.roll(row, LANES - 2 * (block + 1), 1), (LEVELS, LANES))
            for bit in (1, 2, 4, 8):
                row = jnp.where(depth & bit != 0, pltpu.roll(row, LANES - 8 * bit, 1), row)
            return row

        def ns(out, inn):
            return (inn, out) if side == 0 else (out, inn)

        def five(own, halo, out, inn):
            return (own, east_of(own, halo, lane), west_of(own, halo, lane), *ns(out, inn))

        def sides_of(u, uh, p, ph):
            west, east = slopes(u, p)
            west_halo, east_halo = slopes(uh, ph)
            return east_of(west, west_halo, lane), west_of(east, east_halo, lane)

        def share(v, wet, beyond, p):
            wet = TIME_STEP * wet
            weight = wet * (DIFFUSIVITY + toward * v)
            return (
                weight * beyond[0],
                weight * beyond[1],
                wet * (VISCOSITY * beyond[2]),
                wet * (VISCOSITY * beyond[3] + toward * p),
            )

        def plus(a, b):
            return [x + y for x, y in zip(a, b)]

        ring2 = [value[(2 * i + 1) * LEVELS : (2 * i + 2) * LEVELS] for i in range(4)]
        ring1 = [value[2 * i * LEVELS : (2 * i + 1) * LEVELS] for i in range(4)]
        corner = [unfold(value[ROW_CORNER + i : ROW_CORNER + i + 1]) for i in range(5)]
        edge = [raw_ref[side, i, :, row0, :] for i in range(4)]
        wet0, wet1 = raw_ref[side, 4, :, row0, :], raw_ref[side, 4, :, row1, :]
        p_edge = raw_ref[side, 5, :, row0, :]
        v_halo, wet_halo = (rawh_ref[side, i, :, row0, :] for i in range(2))
        one1 = [one_ref[side, i, :, row1, :] for i in range(4)]
        p_one1 = one_ref[side, 4, :, row1, :]
        wet_ring = value[ROW_WET : ROW_WET + LEVELS]
        ps_ring2, ps_ring1 = value[ROW_PS + 1 : ROW_PS + 2], value[ROW_PS : ROW_PS + 1]
        ps0, ps1 = (ps_ref[pl.ds(first + row, 1), :] for row in (row0, row1))
        ps_halo = psh_ref[side, pl.ds(row0, 1), :]
        cor0 = coriolis_of(jnp.int32(first + row0))
        cor_ring = coriolis_of(jnp.int32(first + row0 + (-1 if side == 0 else 1)))

        p_ring2 = pressure(ring2[0], ring2[1], ps_ring2)
        p_ring1 = pressure(ring1[0], ring1[1], ps_ring1)
        p_corner = pressure(corner[0], corner[1], corner[4][0:1])
        ring = march(
            *(five(ring1[i], corner[i], ring2[i], edge[i]) for i in range(2)),
            (ring1[2], *ns(ring2[2], edge[2])),
            five(ring1[3], corner[3], ring2[3], edge[3]),
            ns(p_ring2, p_edge),
            sides_of(ring1[2], corner[2], p_ring1, p_corner),
            wet_ring, cor_ring,
        )
        added = share(edge[3], wet0, ring1, p_ring1)
        one0 = plus([one_ref[side, i, :, row0, :] for i in range(4)], added)
        one0h = plus(
            [oneh_ref[side, i, :, row0, :] for i in range(4)], share(v_halo, wet_halo, corner, p_corner)
        )
        second0 = march(
            *(five(one0[i], one0h[i], ring[i], one1[i]) for i in range(2)),
            (one0[2], *ns(ring[2], one1[2])),
            five(one0[3], one0h[3], ring[3], one1[3]),
            ns(pressure(ring[0], ring[1], ps_ring1), p_one1),
            sides_of(one0[2], one0h[2], pressure(one0[0], one0[1], ps0), pressure(one0h[0], one0h[1], ps_halo)),
            wet0, cor0,
        )
        second1 = plus(
            [two_ref[side, i, :, row1, :] for i in range(4)],
            share(one1[3], wet1, added, pressure(added[0], added[1], 0.0)),
        )
        second0 = (*second0, pressure(second0[0], second0[1], ps0))
        second1 = (*second1, pressure(second1[0], second1[1], ps1))
        for index, out in enumerate(outs):
            block_ref[side, index, :, side, :] = second0[index]
            block_ref[side, index, :, 1 - side, :] = second1[index]
            pltpu.make_async_copy(
                block_ref.at[side, index], out.at[:, pl.ds(side * (ROWS - 2), 2), :], sems.at[0]
            ).start()

    side_rows(0, south)
    side_rows(1, north)
    pltpu.make_async_copy(block_ref, block_ref, sems.at[0]).wait()
    whole = late_ref.at[:, :, inner]
    pltpu.make_async_copy(whole, whole, sems.at[1]).wait()


def exchanges(lon_count, lat_count):
    def at(lat, lon):
        return (lon % lon_count) * lat_count + lat

    def lat_far(lat, lon):
        if lat == 0:
            return at(0, lon ^ 1)
        if lat == lat_count - 1:
            return at(lat, lon_count - 1 - lon)
        return at(lat + 1 if lat % 2 else lat - 1, lon)

    cells = [(lat, lon) for lat in range(lat_count) for lon in range(lon_count)]
    lon_near = [(at(a, o), at(a, o ^ 1)) for a, o in cells]
    lon_far = [(at(a, o), at(a, o + 1 if o % 2 else o - 1)) for a, o in cells]
    lat_near = [(at(a, o), at(a ^ 1, o)) for a, o in cells]
    return lon_near, lon_far, lat_near, [(at(a, o), lat_far(a, o)) for a, o in cells]


def swap(value, pairs):
    return lax.ppermute(value, ("lon", "lat"), pairs)


def on_device(t, s, u, v, ps, wet):
    lon_near, lon_far, lat_near, lat_far = exchanges(lax.axis_size("lon"), lax.axis_size("lat"))
    inputs = (t, s, u, v, ps, wet)
    kept = [pltpu.with_memory_space_constraint(x, pltpu.HBM) for x in inputs]
    cols = jax.ShapeDtypeStruct((COL_ROWS, LANES), jnp.float32)
    rows = jax.ShapeDtypeStruct((ROW_ROWS, LANES), jnp.float32)

    def grant(mib):
        return pltpu.CompilerParams(vmem_limit_bytes=int(mib * 1024 * 1024))

    col_near, col_far = pl.pallas_call(
        pack_columns,
        out_shape=(cols, cols),
        in_specs=[HBM] * 6,
        out_specs=(VMEM, VMEM),
        scratch_shapes=[
            pltpu.VMEM((4, *t.shape), jnp.float32),
            pltpu.VMEM(wet.shape, wet.dtype),
            pltpu.VMEM(ps.shape, jnp.float32),
            pltpu.SemaphoreType.DMA((3,)),
        ],
        compiler_params=grant(6),
    )(*kept)
    block = (LEVELS, 8, LANES)
    row_near, row_far = pl.pallas_call(
        pack_rows,
        out_shape=(rows, rows),
        in_specs=[HBM] * 6,
        out_specs=(VMEM, VMEM),
        scratch_shapes=[
            pltpu.VMEM((2, 4, *block), jnp.float32),
            pltpu.VMEM((2, *block), jnp.int32),
            pltpu.VMEM((ROWS, LANES), jnp.float32),
            pltpu.SemaphoreType.DMA((3,)),
        ],
        compiler_params=grant(4),
    )(*kept)
    got_far = swap(col_far, lon_far)
    got_near = swap(col_near, lon_near)
    row_far, row_near = pl.pallas_call(
        pack_corners,
        out_shape=(rows, rows),
        in_specs=[VMEM] * 4,
        out_specs=(VMEM, VMEM),
        input_output_aliases={2: 0, 3: 1},
        compiler_params=grant(2),
    )(got_far, got_near, row_far, row_near)
    row_far = swap(row_far, lat_far)
    row_near = swap(row_near, lat_near)
    out = jax.ShapeDtypeStruct(t.shape, jnp.float32)

    def blocks(count):
        return jax.ShapeDtypeStruct((2, count, *block), jnp.float32)

    left = jax.ShapeDtypeStruct((5, LEVELS - LATE, ROWS, LANES), jnp.float32)
    plane = pltpu.VMEM((2, ROWS + 16, LANES), jnp.float32)
    *outs, raw, raw_halo, one, one_halo, two, ps_halo, late = pl.pallas_call(
        main_kernel,
        out_shape=(out,) * 5 + (blocks(6), blocks(2), blocks(5), blocks(4), blocks(4), jax.ShapeDtypeStruct((2, 8, LANES), jnp.float32), left),
        in_specs=[VMEM] * 10,
        out_specs=(HBM,) * 5 + (VMEM,) * 7,
        scratch_shapes=[
            plane,
            pltpu.VMEM((2, 4, ROWS + 16, LANES), jnp.float32),
            plane,
            pltpu.VMEM((5, *t.shape), jnp.float32),
            pltpu.SemaphoreType.DMA((len(PARTS),)),
        ],
        compiler_params=grant(12),
    )(*inputs, got_near, got_far, col_near, col_far)
    return pl.pallas_call(
        patch_kernel,
        out_shape=(out,) * 5,
        in_specs=[VMEM] * 10 + [HBM] * 5,
        out_specs=(HBM,) * 5,
        scratch_shapes=[
            pltpu.VMEM((2, 5, LEVELS, 2, LANES), jnp.float32),
            pltpu.SemaphoreType.DMA((2,)),
        ],
        input_output_aliases={10 + i: i for i in range(5)},
        compiler_params=grant(8),
    )(ps, row_far, row_near, raw, raw_halo, one, one_halo, two, ps_halo, late, *outs)


def solution(mesh):
    field = P(None, "lat", "lon")
    return jax.shard_map(
        on_device,
        mesh=mesh,
        in_specs=(field, field, field, field, P("lat", "lon"), field),
        out_specs=(field,) * 5,
        check_vma=False,
    )
```
